32 devices in a mesh: blk: 8 (over z, core), grp: 4 (over y, x).
Axes of the slice: x: 2, y: 2, z: 4, core: 2. Of those that a mesh axis runs over, the one named last changes fastest.
Arguments:
- three_index: bfloat16 [23040, 2048], P('grp', 'blk'), may hold values from -0.359375 to 0.359375
- occ_energy: float32 [32], P('blk'), may hold values from -2 to -0.3
- vir_energy: float32 [64], replicated, may hold values from 0.2 to 3
- aux_count: int32 [4], replicated, may hold values from 1 to 5760, 22528 in all
- occ_count: int32 [8], replicated, may hold values from 1 to 4, 16 in all
Outputs:
- gamma: bfloat16 [23040, 2048], P('grp', 'blk')
The draws below stay inside these ranges and needn't reach their ends.
Inputs may be any that keep to these rules, and one draw needn't show every extreme that they name: `aux_count`: the 4 counts sum to 22528; the largest is exactly 5760. `occ_count`: the 8 counts sum to 16; the largest is exactly 4.
All inputs are finite; a program needn't handle non-finite values.
Results may differ from the reference program's by a relative error of at most 0.018.
Values may be sent and summed in bfloat16 or wider, within the bound.
A program may use at most 64 MiB of HBM per device.

```python
import math
import jax
import jax.numpy as jnp
import numpy as np
from jax import lax

NAUX = 22528
NV = 64
OCC_CAP = 4
NOCC = 16
NOCC_PAD = 32
CAP = 5760
SLOTS = 23040
COLS = 2048
N_BLK = 8
N_GRP = 4


def levels(rng, extent, pieces, smallest, top_value):
    gain, own = 1.0, jax.random.fold_in(rng, 6)
    for dim, shards_of in pieces:
        heights = jnp.exp(jax.random.uniform(jax.random.fold_in(own, dim), (shards_of,), jnp.float32, smallest / len(pieces), top_value / len(pieces)))
        gain = gain * jnp.repeat(heights, extent[dim] // shards_of).reshape([-1 if axis == dim else 1 for axis in range(len(extent))])
    return gain


def length_profile(amount, total, bound, lean):
    weights = [(1 << 20) // math.isqrt(grade ** lean) + 1 for grade in range(2, amount + 1)]
    surplus, given = total - bound - (amount - 1), [1] * (amount - 1)
    while surplus > 0:
        candidates = [i for i in range(amount - 1) if given[i] < bound]
        whole, left = sum([weights[i] for i in candidates]), surplus
        for i in candidates:
            extra = min(bound - given[i], max(1, left * weights[i] // whole), surplus)
            given[i] = given[i] + extra
            surplus = surplus - extra
    return np.array([bound] + given)


def uneven_parts(own_key, count, total, limit, lean):
    if count == 2:
        one = jax.random.randint(own_key, (), max(1, total - limit), min(limit, total - 1) + 1)
        return jnp.stack([one, total - one])
    lengths = jnp.asarray(length_profile(count, total, limit, lean), jnp.int32)
    couples = (count - 1) // 2
    donor, receiver = lengths[1:1 + 2 * couples:2], lengths[2:2 + 2 * couples:2]
    room = jnp.minimum(donor - 1, limit - receiver)
    shifted = jax.random.randint(jax.random.fold_in(own_key, 1), (couples,), 0, 1 << 20) % (room + 1)
    lengths = lengths.at[1:1 + 2 * couples:2].set(donor - shifted).at[2:2 + 2 * couples:2].set(receiver + shifted)
    return lengths[jax.random.permutation(jax.random.fold_in(own_key, 2), count)]


def normal_values(own_key, shape, scale, reach, split=(), held_as=jnp.bfloat16):
    drawn = jax.random.normal(own_key, shape, jnp.float32) * scale
    if len(split) > 0:
        drawn = levels(own_key, shape, split, -0.22, 0.18) * drawn
    return jnp.clip(drawn, min=-reach, max=reach).astype(held_as)


def setup_inputs(seed: int = 0) -> dict:
    keys = jax.random.split(jax.random.key(seed), 6)
    return {
        "three_index": normal_values(keys[0], (SLOTS, COLS), 0.06, 0.359375, ((0, 4), (1, 8))),
        "occ_energy": jnp.clip(-2.0 + 1.7 * jax.random.uniform(keys[1], (NOCC_PAD,), jnp.float32) ** levels(keys[1], (NOCC_PAD,), ((0, 8),), -0.2, 0.2), -2.0, -0.3),
        "vir_energy": jnp.clip(jax.random.uniform(keys[2], (NV,), jnp.float32, 0.2, 3.0), 0.2, 3.0),
        "aux_count": uneven_parts(keys[3], N_GRP, NAUX, CAP, 2).astype(jnp.int32),
        "occ_count": uneven_parts(keys[4], N_BLK, NOCC, OCC_CAP, 2).astype(jnp.int32),
    }


contract_first = (((0,), (0,)), ((), ()))
contract_last = (((1,), (1,)), ((), ()))


def slab_parts(masked, occ_energy, vir_energy, occ_count, slab_index):
    columns = OCC_CAP * NV
    slab_block = lax.dynamic_slice_in_dim(masked, slab_index * columns, columns, 1).astype(jnp.float32)
    slab_energy = lax.dynamic_slice_in_dim(occ_energy, slab_index * OCC_CAP, OCC_CAP, 0)
    col_gap = (slab_energy[:, None] - vir_energy[None, :]).reshape(columns)
    col_live = jnp.repeat(jnp.arange(OCC_CAP) < occ_count[slab_index], NV)
    return slab_block, col_gap, col_live


def amplitude_block(left_parts, right_parts):
    pair_block = lax.dot_general(left_parts[0], right_parts[0], contract_first, precision=lax.Precision.HIGHEST)
    quotient = pair_block / (left_parts[1][:, None] + right_parts[1][None, :])
    both_live = left_parts[2][:, None] & right_parts[2][None, :]
    return jnp.where(both_live, quotient, 0.0).astype(jnp.bfloat16)


def reference(three_index, occ_energy, vir_energy, aux_count, occ_count):
    slot_count = three_index.shape[0] // N_GRP
    aux_live = (jnp.arange(slot_count)[None, :] < aux_count[:, None]).reshape(-1)
    masked = jnp.where(aux_live[:, None], three_index, jnp.zeros((), jnp.bfloat16))

    def slab_of(slab_index):
        return slab_parts(masked, occ_energy, vir_energy, occ_count, slab_index % N_BLK)

    def pair_blocks(slab_index):
        left_parts = slab_of(slab_index)
        return jnp.stack([amplitude_block(left_parts, slab_of(slab_index + offset)) for offset in range(3)])

    slab_ids = jnp.arange(N_BLK, dtype=jnp.int32)
    amplitude = lax.map(pair_blocks, slab_ids)

    def collect_slab(slab_index):
        accumulated = jnp.zeros((masked.shape[0], OCC_CAP * NV), jnp.float32)
        for offset in range(3):
            right_slab = slab_of(slab_index + offset)[0]
            accumulated = accumulated + lax.dot_general(right_slab, amplitude[slab_index, offset].astype(jnp.float32), contract_last, precision=lax.Precision.HIGHEST)
        for offset in (1, 2):
            source = (slab_index - offset) % N_BLK
            left_slab = slab_of(source)[0]
            returned = jnp.dot(left_slab, amplitude[source, offset].astype(jnp.float32), precision=lax.Precision.HIGHEST).astype(jnp.bfloat16)
            accumulated = accumulated + lax.optimization_barrier(returned).astype(jnp.float32)
        return accumulated.astype(jnp.bfloat16)

    gamma = lax.map(collect_slab, slab_ids)
    return jnp.transpose(gamma, (1, 0, 2)).reshape(masked.shape[0], N_BLK * OCC_CAP * NV)
```

```python
import functools

import jax
import jax.numpy as jnp
from jax import lax
from jax.experimental import pallas as pl
from jax.experimental.pallas import tpu as pltpu
from jax.sharding import PartitionSpec as P

UNIT = 128
last_last = (((1,), (1,)), ((), ()))


def dot(a, b):
    return jnp.dot(a, b, preferred_element_type=jnp.float32)


def dot_t(a, b):
    return lax.dot_general(a, b, last_last, preferred_element_type=jnp.float32)


def chunk_rows(rows):
    return max(c for c in range(16, 641, 16) if rows % c == 0)


def kernel(dims, occ_ref, aux_ref, b_ref, raw_ref, out_ref,
           sib, sib_raw, p_own, p_sib, pt_own, pt_sib, pk, bt, gap_row, gap_col,
           nb, nb_gap, vacc, acc, gsib,
           vt_o, rx_o, t_o, vt_u, rx_u, t_u,
           x_sem, m_sem, g_sem, ro_sem, ru_sem, f_sem):
    n_chip, n_grp, U, R, CH, S, D, C, nv = dims
    W = U * UNIT
    Wo = D * S
    NCH = R // CH
    blk = lax.axis_index("blk")
    grp = lax.axis_index("grp")
    chip = blk // 2
    core = blk % 2
    me = grp * 2 + core
    ahead = lax.rem(chip + 1, n_chip)
    behind = lax.rem(chip + n_chip - 1, n_chip)

    def peer(d):
        q = lax.rem(me + d, D)
        return q, {"blk": chip * 2 + q % 2, "grp": q // 2}

    sib_id = {"blk": chip * 2 + 1 - core, "grp": grp}
    ahead_id = {"blk": ahead * 2 + core, "grp": grp}
    behind_id = {"blk": behind * 2 + core, "grp": grp}

    def remote(src, dst, sems, device):
        return pltpu.make_async_remote_copy(
            src_ref=src, dst_ref=dst, send_sem=sems.at[0], recv_sem=sems.at[1],
            device_id=device, device_id_type=pl.DeviceIdType.MESH)

    barrier = pltpu.get_barrier_semaphore()
    for d in range(1, D):
        pl.semaphore_signal(barrier, inc=1, device_id=peer(d)[1], device_id_type=pl.DeviceIdType.MESH)
    for device in (ahead_id, behind_id):
        pl.semaphore_signal(barrier, inc=1, device_id=device, device_id_type=pl.DeviceIdType.MESH)
    pl.semaphore_wait(barrier, D + 1)

    other_half = pl.multiple_of((1 - core) * R, 16)
    my_half = pl.multiple_of(core * R, 16)
    swap = remote(b_ref.at[pl.ds(other_half, R), :], sib, x_sem.at[0], sib_id)
    swap_raw = remote(raw_ref, sib_raw, x_sem.at[1], sib_id)
    swap.start()
    swap_raw.start()

    first = occ_ref[chip * 2] * nv
    total = first + occ_ref[chip * 2 + 1] * nv
    ahead_first = occ_ref[ahead * 2] * nv
    ahead_total = ahead_first + occ_ref[ahead * 2 + 1] * nv
    behind_first = occ_ref[behind * 2] * nv
    behind_total = behind_first + occ_ref[behind * 2 + 1] * nv
    own_base, sib_base = core * first, (1 - core) * first
    own_count = core * (total - first) + (1 - core) * first
    sib_count = total - own_count

    def one_hot(shape, col_dim, base, count):
        i = lax.broadcasted_iota(jnp.int32, shape, col_dim)
        j = lax.broadcasted_iota(jnp.int32, shape, 1 - col_dim)
        return jnp.where((i + base == j) & (i < count), 1.0, 0.0)

    p_own[...] = one_hot((C, W), 0, own_base, own_count).astype(jnp.bfloat16)
    p_sib[...] = one_hot((C, W), 0, sib_base, sib_count).astype(jnp.bfloat16)
    pt_own[...] = one_hot((Wo, C), 1, own_base, own_count).astype(jnp.bfloat16)
    pt_sib[...] = one_hot((Wo, C), 1, sib_base, sib_count).astype(jnp.bfloat16)

    swap_raw.wait()
    exact = functools.partial(jnp.dot, precision=lax.Precision.HIGHEST, preferred_element_type=jnp.float32)
    gap_row[...] = (exact(raw_ref[...], one_hot((C, W), 0, own_base, own_count))
                    + exact(sib_raw[...], one_hot((C, W), 0, sib_base, sib_count)))
    column = jnp.sum(one_hot((Wo, C), 1, own_base, own_count) * raw_ref[0:1, :]
                     + one_hot((Wo, C), 1, sib_base, sib_count) * sib_raw[0:1, :], axis=1, keepdims=True)
    column = jnp.broadcast_to(column, (Wo, UNIT))
    for q in range(D):
        gap_col[q] = column[q * S:(q + 1) * S]
    gap_copies = [remote(gap_row, nb_gap.at[0], g_sem.at[0], ahead_id),
                  remote(gap_row, nb_gap.at[1], g_sem.at[1], behind_id)]
    for copy in gap_copies:
        copy.start()

    aux = aux_ref[grp]
    swap.wait()

    def unit_copies(j):
        return [remote(pk.at[j], nb.at[0, j], m_sem.at[0, j], ahead_id),
                remote(pk.at[j], nb.at[1, j], m_sem.at[1, j], behind_id)]

    def at_chunk(i):
        return pl.ds(pl.multiple_of(i * CH, 16), CH)

    def own_chunk(i):
        return b_ref[pl.ds(pl.multiple_of(core * R + i * CH, 16), CH), :]

    for j in range(U):
        cols = slice(j * UNIT, (j + 1) * UNIT)

        @pl.loop(0, NCH)
        def _(i):
            packed = dot(own_chunk(i), p_own[:, cols]) + dot(sib[at_chunk(i), :], p_sib[:, cols])
            row = lax.broadcasted_iota(jnp.int32, (CH, UNIT), 0) + (core * R + i * CH)
            pk[j, at_chunk(i), :] = jnp.where(row < aux, packed, 0.0).astype(jnp.bfloat16)

        for copy in unit_copies(j):
            copy.start()

    @pl.loop(0, NCH)
    def _(i):
        bt[i] = (dot_t(pt_own[...], own_chunk(i)) + dot_t(pt_sib[...], sib[at_chunk(i), :])).astype(jnp.bfloat16)

    def pk_chunk(i):
        return jnp.concatenate([pk[j, at_chunk(i), :] for j in range(U)], axis=1)

    def nb_chunk(j, i):
        return jnp.concatenate([nb[0, j, at_chunk(i), :], nb[1, j, at_chunk(i), :]], axis=1)

    def pair_sums(vt, load, N):
        vacc[:, :N] = jnp.zeros((Wo, N), jnp.float32)

        @pl.loop(0, NCH)
        def _(i):
            vacc[:, :N] += dot(bt[i], load(i))

        for q in range(D):
            vt[q] = vacc[q * S:(q + 1) * S, :N].astype(jnp.bfloat16)

    def reduce(vt, rx, t, sems, N, gap_u, valid):
        parts = []
        for d in range(1, D):
            q, device = peer(d)
            parts.append(remote(vt.at[q], rx.at[d - 1], sems.at[0, d - 1], device))
        for copy in parts:
            copy.start()
        value = vt[me].astype(jnp.float32)
        for d, copy in enumerate(parts):
            copy.wait_recv()
            value = value + rx[d].astype(jnp.float32)
        w = lax.broadcasted_iota(jnp.int32, (S, N), 0) + me * S
        u = lax.broadcasted_iota(jnp.int32, (S, N), 1)
        gap_w = jnp.concatenate([gap_col[me]] * (N // UNIT), axis=1)
        quotient = value / (gap_w + gap_u)
        t[me] = jnp.where(valid(u, w) & (w < total), quotient, 0.0).astype(jnp.bfloat16)
        backs = []
        for d in range(1, D):
            backs.append(remote(t.at[me], t.at[me], sems.at[1, d - 1], peer(d)[1]))
        for copy in backs:
            copy.start()
        for copy in backs:
            copy.wait_recv()
        for copy in parts + backs:
            copy.wait_send()

    pair_sums(vt_o, pk_chunk, W)
    reduce(vt_o, rx_o, t_o, ro_sem, W, gap_row[0:1, :], lambda u, w: u < total)

    @pl.loop(0, NCH)
    def _(i):
        acc[at_chunk(i), :] = dot_t(pk_chunk(i), t_o[...].reshape(Wo, W))

    for copy in gap_copies:
        copy.wait()

    for j in range(U):
        for copy in unit_copies(j):
            copy.wait_recv()
        pair_sums(vt_u.at[j], lambda i: nb_chunk(j, i), 2 * UNIT)
        cols = slice(j * UNIT, (j + 1) * UNIT)
        gap_u = jnp.concatenate([nb_gap[0, 0:1, cols], nb_gap[1, 0:1, cols]], axis=1)

        def valid(u, w):
            shifted = u + j * UNIT
            from_behind = (shifted < behind_total) & ((shifted >= behind_first) | (w < first))
            place = shifted - UNIT
            from_ahead = (place < ahead_total) & ((place < ahead_first) | (w >= first))
            return ((u < UNIT) & from_behind) | ((u >= UNIT) & from_ahead)

        reduce(vt_u.at[j], rx_u.at[j], t_u.at[j], ru_sem.at[j], 2 * UNIT, gap_u, valid)
        if j < U - 1:
            @pl.loop(0, NCH)
            def _(i):
                acc[at_chunk(i), :] += dot_t(nb_chunk(j, i), t_u[j].reshape(Wo, 2 * UNIT))

    def back(i):
        rows = pl.ds(pl.multiple_of(core * R + i * CH, 16), CH)
        return remote(gsib.at[at_chunk(i), :], out_ref.at[rows, :], f_sem.at[i], sib_id)

    @pl.loop(0, NCH)
    def _(i):
        value = acc[at_chunk(i), :] + dot_t(nb_chunk(U - 1, i), t_u[U - 1].reshape(Wo, 2 * UNIT))
        value = value.astype(jnp.bfloat16)
        gsib[at_chunk(i), :] = dot(value, pt_sib[...]).astype(jnp.bfloat16)
        back(i).start()
        rows = pl.ds(pl.multiple_of(core * R + i * CH, 16), CH)
        out_ref[rows, :] = dot(value, pt_own[...]).astype(jnp.bfloat16)

    @pl.loop(0, NCH)
    def _(i):
        back(i).wait()

    for j in range(U):
        for copy in unit_copies(j):
            copy.wait_send()


def call(n_chip, n_grp, U, nv, ident, occ_count, aux_count, block, raw):
    rows, C = block.shape
    R = rows // 2
    CH = chunk_rows(R)
    D = 2 * n_grp
    W = U * UNIT
    S = -(-W // (D * 16)) * 16
    Wo = D * S
    N = 2 * UNIT
    dims = (n_chip, n_grp, U, R, CH, S, D, C, nv)
    bf, f32 = jnp.bfloat16, jnp.float32
    vm, dma = pltpu.VMEM, pltpu.SemaphoreType.DMA
    scratch = [
        vm((R, C), bf), vm((8, C), f32), vm((C, W), bf), vm((C, W), bf), vm((Wo, C), bf), vm((Wo, C), bf),
        vm((U, R, UNIT), bf), vm((R // CH, Wo, CH), bf), vm((8, W), f32), vm((D, S, UNIT), f32),
        vm((2, U, R, UNIT), bf), vm((2, 8, W), f32), vm((Wo, W), f32), vm((R, Wo), f32), vm((R, C), bf),
        vm((D, S, W), bf), vm((D, S, W), bf), vm((D, S, W), bf),
        vm((U, D, S, N), bf), vm((U, D, S, N), bf), vm((U, D, S, N), bf),
        dma((2, 2)), dma((2, U, 2)), dma((2, 2)), dma((2, D, 2)), dma((U, 2, D, 2)), dma((R // CH, 2)),
    ]
    smem = pl.BlockSpec(memory_space=pltpu.SMEM)
    vmem = pl.BlockSpec(memory_space=pltpu.VMEM)
    return pl.pallas_call(
        functools.partial(kernel, dims),
        out_shape=jax.ShapeDtypeStruct((rows, C), bf),
        in_specs=[smem, smem, vmem, vmem],
        out_specs=vmem,
        scratch_shapes=scratch,
        compiler_params=pltpu.CompilerParams(
            collective_id=ident, has_side_effects=True, vmem_limit_bytes=56 * 1024 * 1024),
        cost_estimate=pl.CostEstimate(flops=12 * R * W * Wo, bytes_accessed=4 * rows * C, transcendentals=0),
    )(occ_count, aux_count, block, raw)


def solution(mesh):
    n_chip, n_grp = mesh.shape["blk"] // 2, mesh.shape["grp"]

    def per_device(three_index, occ_energy, vir_energy, aux_count, occ_count):
        C, nv = three_index.shape[1], vir_energy.shape[0]
        gap = (occ_energy[:, None] - vir_energy[None, :]).reshape(1, C)
        raw = jnp.broadcast_to(gap, (8, C))
        most = jnp.max(occ_count[0::2] + occ_count[1::2]) * nv
        full = 2 * C // UNIT
        return lax.cond(
            most <= (full - 1) * UNIT,
            functools.partial(call, n_chip, n_grp, full - 1, nv, 1),
            functools.partial(call, n_chip, n_grp, full, nv, 2),
            occ_count, aux_count, three_index, raw)

    in_specs = (P("grp", "blk"), P("blk"), P(), P(), P())
    return jax.shard_map(
        per_device, mesh=mesh, in_specs=in_specs, out_specs=P("grp", "blk"), check_vma=False)
```

```python
import functools

import jax
import jax.numpy as jnp
from jax import lax
from jax.experimental import pallas as pl
from jax.experimental.pallas import tpu as pltpu
from jax.sharding import PartitionSpec as P

UNIT = 128
last_last = (((1,), (1,)), ((), ()))


def dot(a, b):
    return jnp.dot(a, b, preferred_element_type=jnp.float32)


def dot_t(a, b):
    return lax.dot_general(a, b, last_last, preferred_element_type=jnp.float32)


def chunk_rows(rows):
    return max(c for c in range(16, 641, 16) if rows % c == 0)


def kernel(dims, occ_ref, aux_ref, energy_ref, vir_ref, b_ref, out_ref,
           raw_ref, sib, sib_raw, p_own, p_sib, pt_own, pt_sib, pk, bt, gap_row, gap_col,
           nb, nb_gap, vacc, acc, gsib,
           vt_o, rx_o, t_o, vt_u, rx_u, t_u,
           x_sem, m_sem, w_sem, g_sem, ro_sem, ru_sem, f_sem):
    n_chip, n_grp, edge_units, inner_units, R, CH, S, D, C, nv = dims
    U = max(edge_units, inner_units)
    relay = n_chip == 4
    W = U * UNIT
    Wo = D * S
    NCH = R // CH
    blk = lax.axis_index("blk")
    grp = lax.axis_index("grp")
    chip = blk // 2
    core = blk % 2
    me = grp * 2 + core
    ahead = lax.rem(chip + 1, n_chip)
    behind = lax.rem(chip + n_chip - 1, n_chip)

    def peer(d):
        q = lax.rem(me + d, D)
        return q, {"blk": chip * 2 + q % 2, "grp": q // 2}

    sib_id = {"blk": chip * 2 + 1 - core, "grp": grp}
    ahead_id = {"blk": ahead * 2 + core, "grp": grp}
    behind_id = {"blk": behind * 2 + core, "grp": grp}

    def remote(src, dst, sems, device):
        return pltpu.make_async_remote_copy(
            src_ref=src, dst_ref=dst, send_sem=sems.at[0], recv_sem=sems.at[1],
            device_id=device, device_id_type=pl.DeviceIdType.MESH)

    exact = functools.partial(jnp.dot, precision=lax.Precision.HIGHEST, preferred_element_type=jnp.float32)
    barrier = pltpu.get_barrier_semaphore()
    for d in range(1, D):
        pl.semaphore_signal(barrier, inc=1, device_id=peer(d)[1], device_id_type=pl.DeviceIdType.MESH)
    across_id = {"blk": lax.rem(chip + 2, n_chip) * 2 + core, "grp": grp}
    others = (ahead_id, behind_id) + ((across_id,) if relay else ())
    for device in others:
        pl.semaphore_signal(barrier, inc=1, device_id=device, device_id_type=pl.DeviceIdType.MESH)

    lane = lax.broadcasted_iota(jnp.int32, (8, C), 1)
    spread = jnp.where(lax.broadcasted_iota(jnp.int32, (nv, C), 1) % nv
                       == lax.broadcasted_iota(jnp.int32, (nv, C), 0), 1.0, 0.0)
    gap = -exact(jnp.broadcast_to(vir_ref[...], (8, nv)), spread)
    for k in range(C // nv):
        gap = gap + jnp.where((lane >= k * nv) & (lane < (k + 1) * nv), energy_ref[k], 0.0)
    raw_ref[...] = gap
    pl.semaphore_wait(barrier, D - 1 + len(others))

    other_half = pl.multiple_of((1 - core) * R, 16)
    my_half = pl.multiple_of(core * R, 16)
    swap = remote(b_ref.at[pl.ds(other_half, R), :], sib, x_sem.at[0], sib_id)
    swap_raw = remote(raw_ref, sib_raw, x_sem.at[1], sib_id)
    swap.start()
    swap_raw.start()

    first = occ_ref[chip * 2] * nv
    total = first + occ_ref[chip * 2 + 1] * nv
    ahead_first = occ_ref[ahead * 2] * nv
    ahead_total = ahead_first + occ_ref[ahead * 2 + 1] * nv
    behind_first = occ_ref[behind * 2] * nv
    behind_total = behind_first + occ_ref[behind * 2 + 1] * nv
    own_base, sib_base = core * first, (1 - core) * first
    own_count = core * (total - first) + (1 - core) * first
    sib_count = total - own_count

    def one_hot(shape, col_dim, base, count):
        i = lax.broadcasted_iota(jnp.int32, shape, col_dim)
        j = lax.broadcasted_iota(jnp.int32, shape, 1 - col_dim)
        return jnp.where((i + base == j) & (i < count), 1.0, 0.0)

    p_own[...] = one_hot((C, W), 0, own_base, own_count).astype(jnp.bfloat16)
    p_sib[...] = one_hot((C, W), 0, sib_base, sib_count).astype(jnp.bfloat16)
    pt_own[...] = one_hot((Wo, C), 1, own_base, own_count).astype(jnp.bfloat16)
    pt_sib[...] = one_hot((Wo, C), 1, sib_base, sib_count).astype(jnp.bfloat16)

    swap_raw.wait()
    gap_row[...] = (exact(raw_ref[...], one_hot((C, W), 0, own_base, own_count))
                    + exact(sib_raw[...], one_hot((C, W), 0, sib_base, sib_count)))
    column = jnp.sum(one_hot((Wo, C), 1, own_base, own_count) * raw_ref[0:1, :]
                     + one_hot((Wo, C), 1, sib_base, sib_count) * sib_raw[0:1, :], axis=1, keepdims=True)
    column = jnp.broadcast_to(column, (Wo, UNIT))
    for q in range(D):
        gap_col[q] = column[q * S:(q + 1) * S]
    gap_copies = [remote(gap_row, nb_gap.at[0], g_sem.at[0], ahead_id),
                  remote(gap_row, nb_gap.at[1], g_sem.at[1], behind_id)]
    for copy in gap_copies:
        copy.start()

    aux = aux_ref[grp]
    swap.wait()

    def up(j):
        return remote(pk.at[j], nb.at[0, j], m_sem.at[0, j], ahead_id)

    def down(j):
        return remote(pk.at[j], nb.at[1, j], m_sem.at[1, j], behind_id)

    def relay_up(j):
        return remote(nb.at[0, j], nb.at[1, j], w_sem.at[0, j], across_id)

    def relay_down(j):
        return remote(nb.at[1, j], nb.at[0, j], w_sem.at[1, j], across_id)

    def holds(j, where):
        at_end = (where == 0) | (where == n_chip - 1)
        return ((j < edge_units) & at_end) | ((j < inner_units) & jnp.logical_not(at_end))

    def sends_up(j):
        return holds(j, chip) & (chip != n_chip - 1) if relay else holds(j, chip)

    def sends_down(j):
        return holds(j, chip) & (chip != 0) if relay else holds(j, chip)

    def at_chunk(i):
        return pl.ds(pl.multiple_of(i * CH, 16), CH)

    def own_chunk(i):
        return b_ref[pl.ds(pl.multiple_of(core * R + i * CH, 16), CH), :]

    for j in range(U):
        cols = slice(j * UNIT, (j + 1) * UNIT)

        @pl.loop(0, NCH)
        def _(i):
            packed = dot(own_chunk(i), p_own[:, cols]) + dot(sib[at_chunk(i), :], p_sib[:, cols])
            row = lax.broadcasted_iota(jnp.int32, (CH, UNIT), 0) + (core * R + i * CH)
            pk[j, at_chunk(i), :] = jnp.where(row < aux, packed, 0.0).astype(jnp.bfloat16)

        @pl.when(sends_up(j))
        def _():
            up(j).start()

        @pl.when(sends_down(j))
        def _():
            down(j).start()

        if j >= min(edge_units, inner_units):
            @pl.when(jnp.logical_not(holds(j, behind)))
            def _():
                nb[0, j] = jnp.zeros((R, UNIT), jnp.bfloat16)

            @pl.when(jnp.logical_not(holds(j, ahead)))
            def _():
                nb[1, j] = jnp.zeros((R, UNIT), jnp.bfloat16)

    @pl.loop(0, NCH)
    def _(i):
        bt[i] = (dot_t(pt_own[...], own_chunk(i)) + dot_t(pt_sib[...], sib[at_chunk(i), :])).astype(jnp.bfloat16)

    def pk_chunk(i):
        return jnp.concatenate([pk[j, at_chunk(i), :] for j in range(U)], axis=1)

    def nb_chunk(j, i):
        return jnp.concatenate([nb[0, j, at_chunk(i), :], nb[1, j, at_chunk(i), :]], axis=1)

    def pair_sums(vt, load, N):
        vacc[:, :N] = jnp.zeros((Wo, N), jnp.float32)

        @pl.loop(0, NCH)
        def _(i):
            vacc[:, :N] += dot(bt[i], load(i))

        for q in range(D):
            vt[q] = vacc[q * S:(q + 1) * S, :N].astype(jnp.bfloat16)

    def reduce(vt, rx, t, sems, N, gap_u, valid):
        parts = []
        for d in range(1, D):
            q, device = peer(d)
            parts.append(remote(vt.at[q], rx.at[d - 1], sems.at[0, d - 1], device))
        for copy in parts:
            copy.start()
        value = vt[me].astype(jnp.float32)
        for d, copy in enumerate(parts):
            copy.wait_recv()
            value = value + rx[d].astype(jnp.float32)
        w = lax.broadcasted_iota(jnp.int32, (S, N), 0) + me * S
        u = lax.broadcasted_iota(jnp.int32, (S, N), 1)
        gap_w = jnp.concatenate([gap_col[me]] * (N // UNIT), axis=1)
        quotient = value / (gap_w + gap_u)
        t[me] = jnp.where(valid(u, w) & (w < total), quotient, 0.0).astype(jnp.bfloat16)
        backs = []
        for d in range(1, D):
            backs.append(remote(t.at[me], t.at[me], sems.at[1, d - 1], peer(d)[1]))
        for copy in backs:
            copy.start()
        for copy in backs:
            copy.wait_recv()
        for copy in parts + backs:
            copy.wait_send()

    pair_sums(vt_o, pk_chunk, W)
    reduce(vt_o, rx_o, t_o, ro_sem, W, gap_row[0:1, :], lambda u, w: u < total)

    @pl.loop(0, NCH)
    def _(i):
        acc[at_chunk(i), :] = dot_t(pk_chunk(i), t_o[...].reshape(Wo, W))

    for copy in gap_copies:
        copy.wait()

    for j in range(U):
        def arrived_behind():
            if relay:
                @pl.when(holds(j, behind) & (chip != 0))
                def _():
                    up(j).wait_recv()

                @pl.when(holds(j, behind) & (chip == 0))
                def _():
                    relay_down(j).wait_recv()
            else:
                @pl.when(holds(j, behind))
                def _():
                    up(j).wait_recv()

        def arrived_ahead():
            if relay:
                @pl.when(holds(j, ahead) & (chip != n_chip - 1))
                def _():
                    down(j).wait_recv()

                @pl.when(holds(j, ahead) & (chip == n_chip - 1))
                def _():
                    relay_up(j).wait_recv()
            else:
                @pl.when(holds(j, ahead))
                def _():
                    down(j).wait_recv()

        if relay:
            @pl.when(chip == n_chip - 2)
            def _():
                arrived_ahead()
                if j < edge_units:
                    relay_down(j).start()
                arrived_behind()

            @pl.when(chip != n_chip - 2)
            def _():
                arrived_behind()
                if j < edge_units:
                    @pl.when(chip == 1)
                    def _():
                        relay_up(j).start()
                arrived_ahead()
        else:
            arrived_behind()
            arrived_ahead()
        pair_sums(vt_u.at[j], lambda i: nb_chunk(j, i), 2 * UNIT)
        cols = slice(j * UNIT, (j + 1) * UNIT)
        gap_u = jnp.concatenate([nb_gap[0, 0:1, cols], nb_gap[1, 0:1, cols]], axis=1)

        def valid(u, w):
            shifted = u + j * UNIT
            from_behind = (shifted < behind_total) & ((shifted >= behind_first) | (w < first))
            place = shifted - UNIT
            from_ahead = (place < ahead_total) & ((place < ahead_first) | (w >= first))
            return ((u < UNIT) & from_behind) | ((u >= UNIT) & from_ahead)

        reduce(vt_u.at[j], rx_u.at[j], t_u.at[j], ru_sem.at[j], 2 * UNIT, gap_u, valid)
        if j < U - 1:
            @pl.loop(0, NCH)
            def _(i):
                acc[at_chunk(i), :] += dot_t(nb_chunk(j, i), t_u[j].reshape(Wo, 2 * UNIT))

    def back(i):
        rows = pl.ds(pl.multiple_of(core * R + i * CH, 16), CH)
        return remote(gsib.at[at_chunk(i), :], out_ref.at[rows, :], f_sem.at[i], sib_id)

    @pl.loop(0, NCH)
    def _(i):
        value = acc[at_chunk(i), :] + dot_t(nb_chunk(U - 1, i), t_u[U - 1].reshape(Wo, 2 * UNIT))
        value = value.astype(jnp.bfloat16)
        gsib[at_chunk(i), :] = dot(value, pt_sib[...]).astype(jnp.bfloat16)
        back(i).start()
        rows = pl.ds(pl.multiple_of(core * R + i * CH, 16), CH)
        out_ref[rows, :] = dot(value, pt_own[...]).astype(jnp.bfloat16)

    @pl.loop(0, NCH)
    def _(i):
        back(i).wait()

    for j in range(U):
        @pl.when(sends_up(j))
        def _():
            up(j).wait_send()

        @pl.when(sends_down(j))
        def _():
            down(j).wait_send()

        if relay and j < edge_units:
            @pl.when(chip == 1)
            def _():
                relay_up(j).wait_send()

            @pl.when(chip == n_chip - 2)
            def _():
                relay_down(j).wait_send()


def call(n_chip, n_grp, edge_units, inner_units, ident, occ_count, aux_count, energy, vir, block):
    U, nv = max(edge_units, inner_units), vir.shape[1]
    rows, C = block.shape
    R = rows // 2
    CH = chunk_rows(R)
    D = 2 * n_grp
    W = U * UNIT
    S = -(-W // (D * 16)) * 16
    Wo = D * S
    N = 2 * UNIT
    dims = (n_chip, n_grp, edge_units, inner_units, R, CH, S, D, C, nv)
    bf, f32 = jnp.bfloat16, jnp.float32
    vm, dma = pltpu.VMEM, pltpu.SemaphoreType.DMA
    scratch = [
        vm((8, C), f32), vm((R, C), bf), vm((8, C), f32), vm((C, W), bf), vm((C, W), bf), vm((Wo, C), bf), vm((Wo, C), bf),
        vm((U, R, UNIT), bf), vm((R // CH, Wo, CH), bf), vm((8, W), f32), vm((D, S, UNIT), f32),
        vm((2, U, R, UNIT), bf), vm((2, 8, W), f32), vm((Wo, W), f32), vm((R, Wo), f32), vm((R, C), bf),
        vm((D, S, W), bf), vm((D, S, W), bf), vm((D, S, W), bf),
        vm((U, D, S, N), bf), vm((U, D, S, N), bf), vm((U, D, S, N), bf),
        dma((2, 2)), dma((2, U, 2)), dma((2, U, 2)), dma((2, 2)), dma((2, D, 2)), dma((U, 2, D, 2)), dma((R // CH, 2)),
    ]
    smem = pl.BlockSpec(memory_space=pltpu.SMEM)
    vmem = pl.BlockSpec(memory_space=pltpu.VMEM)
    return pl.pallas_call(
        functools.partial(kernel, dims),
        out_shape=jax.ShapeDtypeStruct((rows, C), bf),
        in_specs=[smem, smem, smem, vmem, vmem],
        out_specs=vmem,
        scratch_shapes=scratch,
        compiler_params=pltpu.CompilerParams(
            collective_id=ident, has_side_effects=True, vmem_limit_bytes=56 * 1024 * 1024),
        cost_estimate=pl.CostEstimate(flops=12 * R * W * Wo, bytes_accessed=4 * rows * C, transcendentals=0),
    )(occ_count, aux_count, energy, vir, block)


def solution(mesh):
    n_chip, n_grp = mesh.shape["blk"] // 2, mesh.shape["grp"]

    def per_device(three_index, occ_energy, vir_energy, aux_count, occ_count):
        C, nv = three_index.shape[1], vir_energy.shape[0]
        full = 2 * C // UNIT
        member = (jnp.arange(2 * n_chip)[None, :] // 2) == jnp.arange(n_chip)[:, None]
        columns = jnp.sum(jnp.where(member, occ_count[None, :], 0), axis=1) * nv
        at_end = (jnp.arange(n_chip) == 0) | (jnp.arange(n_chip) == n_chip - 1)
        edge_most = jnp.max(jnp.where(at_end, columns, 0))
        inner_most = jnp.max(jnp.where(at_end, 0, columns))
        if n_chip == 4:
            plans = [(full - 2, full - 1), (full - 1, full - 2), (full - 1, full - 1),
                     (full - 2, full), (full, full - 2), (full, full)]
        else:
            plans = [(full - 1, full - 1), (full, full)]
        choice = jnp.int32(len(plans) - 1)
        for i in reversed(range(len(plans) - 1)):
            fits = (edge_most <= plans[i][0] * UNIT) & (inner_most <= plans[i][1] * UNIT)
            choice = jnp.where(fits, i, choice)
        return lax.switch(
            choice,
            [functools.partial(call, n_chip, n_grp, *plan, i + 1) for i, plan in enumerate(plans)],
            occ_count, aux_count, occ_energy, vir_energy.reshape(1, nv), three_index)

    in_specs = (P("grp", "blk"), P("blk"), P(), P(), P())
    return jax.shard_map(
        per_device, mesh=mesh, in_specs=in_specs, out_specs=P("grp", "blk"), check_vma=False)
```

```python
import functools

import jax
import jax.numpy as jnp
from jax import lax
from jax.experimental import pallas as pl
from jax.experimental.pallas import tpu as pltpu
from jax.sharding import PartitionSpec as P

UNIT = 128
last_last = (((1,), (1,)), ((), ()))


def dot(a, b):
    return jnp.dot(a, b, preferred_element_type=jnp.float32)


def dot_t(a, b):
    return lax.dot_general(a, b, last_last, preferred_element_type=jnp.float32)


def chunk_rows(rows):
    return max(c for c in range(16, 641, 16) if rows % c == 0)


def kernel(dims, occ_ref, aux_ref, energy_ref, vir_ref, b_ref, out_ref,
           raw_ref, sib, sib_raw, p_own, p_sib, pt_own, pt_sib, pk, half, bt, gap_row, gap_col,
           nb, nb_half, nb_gap, vacc, acc, gsib,
           vt_o, rx_o, t_o, vt_u, rx_u, t_u,
           x_sem, m_sem, w_sem, g_sem, ro_sem, ru_sem, f_sem):
    n_chip, n_grp, edge_halves, inner_halves, R, CH, S, D, C, nv = dims
    U = -(-max(edge_halves, inner_halves) // 2)
    H = R // 2
    HCH = H // CH
    relay = n_chip == 4
    W = U * UNIT
    Wo = D * S
    NCH = R // CH
    blk = lax.axis_index("blk")
    grp = lax.axis_index("grp")
    chip = blk // 2
    core = blk % 2
    me = grp * 2 + core
    ahead = lax.rem(chip + 1, n_chip)
    behind = lax.rem(chip + n_chip - 1, n_chip)

    def peer(d):
        q = lax.rem(me + d, D)
        return q, {"blk": chip * 2 + q % 2, "grp": q // 2}

    sib_id = {"blk": chip * 2 + 1 - core, "grp": grp}
    ahead_id = {"blk": ahead * 2 + core, "grp": grp}
    behind_id = {"blk": behind * 2 + core, "grp": grp}

    def remote(src, dst, sems, device):
        return pltpu.make_async_remote_copy(
            src_ref=src, dst_ref=dst, send_sem=sems.at[0], recv_sem=sems.at[1],
            device_id=device, device_id_type=pl.DeviceIdType.MESH)

    exact = functools.partial(jnp.dot, precision=lax.Precision.HIGHEST, preferred_element_type=jnp.float32)
    barrier = pltpu.get_barrier_semaphore()
    for d in range(1, D):
        pl.semaphore_signal(barrier, inc=1, device_id=peer(d)[1], device_id_type=pl.DeviceIdType.MESH)
    across_id = {"blk": lax.rem(chip + 2, n_chip) * 2 + core, "grp": grp}
    others = (ahead_id, behind_id) + ((across_id,) if relay else ())
    for device in others:
        pl.semaphore_signal(barrier, inc=1, device_id=device, device_id_type=pl.DeviceIdType.MESH)

    lane = lax.broadcasted_iota(jnp.int32, (8, C), 1)
    spread = jnp.where(lax.broadcasted_iota(jnp.int32, (nv, C), 1) % nv
                       == lax.broadcasted_iota(jnp.int32, (nv, C), 0), 1.0, 0.0)
    gap = -exact(jnp.broadcast_to(vir_ref[...], (8, nv)), spread)
    for k in range(C // nv):
        gap = gap + jnp.where((lane >= k * nv) & (lane < (k + 1) * nv), energy_ref[k], 0.0)
    raw_ref[...] = gap
    pl.semaphore_wait(barrier, D - 1 + len(others))

    other_half = pl.multiple_of((1 - core) * R, 16)
    my_half = pl.multiple_of(core * R, 16)
    swap = remote(b_ref.at[pl.ds(other_half, R), :], sib, x_sem.at[0], sib_id)
    swap_raw = remote(raw_ref, sib_raw, x_sem.at[1], sib_id)
    swap.start()
    swap_raw.start()

    first = occ_ref[chip * 2] * nv
    total = first + occ_ref[chip * 2 + 1] * nv
    ahead_first = occ_ref[ahead * 2] * nv
    ahead_total = ahead_first + occ_ref[ahead * 2 + 1] * nv
    behind_first = occ_ref[behind * 2] * nv
    behind_total = behind_first + occ_ref[behind * 2 + 1] * nv
    own_base, sib_base = core * first, (1 - core) * first
    own_count = core * (total - first) + (1 - core) * first
    sib_count = total - own_count

    def one_hot(shape, col_dim, base, count):
        i = lax.broadcasted_iota(jnp.int32, shape, col_dim)
        j = lax.broadcasted_iota(jnp.int32, shape, 1 - col_dim)
        return jnp.where((i + base == j) & (i < count), 1.0, 0.0)

    p_own[...] = one_hot((C, W), 0, own_base, own_count).astype(jnp.bfloat16)
    p_sib[...] = one_hot((C, W), 0, sib_base, sib_count).astype(jnp.bfloat16)
    pt_own[...] = one_hot((Wo, C), 1, own_base, own_count).astype(jnp.bfloat16)
    pt_sib[...] = one_hot((Wo, C), 1, sib_base, sib_count).astype(jnp.bfloat16)

    swap_raw.wait()
    gap_row[...] = (exact(raw_ref[...], one_hot((C, W), 0, own_base, own_count))
                    + exact(sib_raw[...], one_hot((C, W), 0, sib_base, sib_count)))
    column = jnp.sum(one_hot((Wo, C), 1, own_base, own_count) * raw_ref[0:1, :]
                     + one_hot((Wo, C), 1, sib_base, sib_count) * sib_raw[0:1, :], axis=1, keepdims=True)
    column = jnp.broadcast_to(column, (Wo, UNIT))
    for q in range(D):
        gap_col[q] = column[q * S:(q + 1) * S]
    gap_copies = [remote(gap_row, nb_gap.at[0], g_sem.at[0], ahead_id),
                  remote(gap_row, nb_gap.at[1], g_sem.at[1], behind_id)]
    for copy in gap_copies:
        copy.start()

    aux = aux_ref[grp]
    swap.wait()

    def up(j, whole):
        src, dst = (pk.at[j], nb.at[0, j]) if whole else (half, nb_half.at[0])
        return remote(src, dst, m_sem.at[0, j], ahead_id)

    def down(j, whole):
        src, dst = (pk.at[j], nb.at[1, j]) if whole else (half, nb_half.at[1])
        return remote(src, dst, m_sem.at[1, j], behind_id)

    def relay_up(j, whole):
        src, dst = (nb.at[0, j], nb.at[1, j]) if whole else (nb_half.at[0], nb_half.at[1])
        return remote(src, dst, w_sem.at[0, j], across_id)

    def relay_down(j, whole):
        src, dst = (nb.at[1, j], nb.at[0, j]) if whole else (nb_half.at[1], nb_half.at[0])
        return remote(src, dst, w_sem.at[1, j], across_id)

    def has(j, halves, whole):
        return 2 * j + 2 <= halves if whole else 2 * j + 1 == halves

    def forms(j):
        return [w for w in (True, False) if has(j, edge_halves, w) or has(j, inner_halves, w)]

    def holds(j, whole, where):
        at_end = (where == 0) | (where == n_chip - 1)
        return (has(j, edge_halves, whole) & at_end) | (has(j, inner_halves, whole) & jnp.logical_not(at_end))

    def sends_up(j, whole):
        return holds(j, whole, chip) & (chip != n_chip - 1) if relay else holds(j, whole, chip)

    def sends_down(j, whole):
        return holds(j, whole, chip) & (chip != 0) if relay else holds(j, whole, chip)

    def at_chunk(i):
        return pl.ds(pl.multiple_of(i * CH, 16), CH)

    def own_chunk(i):
        return b_ref[pl.ds(pl.multiple_of(core * R + i * CH, 16), CH), :]

    def masked(i, value):
        row = lax.broadcasted_iota(jnp.int32, (CH, UNIT), 0) + (core * R + i * CH)
        return jnp.where(row < aux, value, 0.0)

    def packed(i, j):
        cols = slice(j * UNIT, (j + 1) * UNIT)
        return masked(i, dot(own_chunk(i), p_own[:, cols]) + dot(sib[at_chunk(i), :], p_sib[:, cols]))

    src_lane = lax.broadcasted_iota(jnp.int32, (UNIT, UNIT), 0)
    dst_lane = lax.broadcasted_iota(jnp.int32, (UNIT, UNIT), 1)
    low = dst_lane < UNIT // 2
    raised = jnp.where(src_lane == dst_lane - UNIT // 2, 1.0, 0.0).astype(jnp.bfloat16)
    kept = jnp.where((src_lane == dst_lane) & low, 1.0, 0.0).astype(jnp.bfloat16)
    lowered = jnp.where(src_lane == dst_lane + UNIT // 2, 1.0, 0.0).astype(jnp.bfloat16)

    for j in range(U):
        @pl.loop(0, NCH)
        def _(i):
            pk[j, at_chunk(i), :] = packed(i, j).astype(jnp.bfloat16)

        for whole in forms(j):
            if not whole:
                @pl.loop(0, HCH)
                def _(i):
                    upper = dot(pk[j, at_chunk(i), :], kept)
                    lower = dot(pk[j, at_chunk(i + HCH), :], raised)
                    half[at_chunk(i), :] = (upper + lower).astype(jnp.bfloat16)

            @pl.when(sends_up(j, whole))
            def _():
                up(j, whole).start()

            @pl.when(sends_down(j, whole))
            def _():
                down(j, whole).start()

        def empty(where):
            return jnp.logical_not(holds(j, True, where) | holds(j, False, where))

        if 2 * j >= min(edge_halves, inner_halves):
            @pl.when(empty(behind))
            def _():
                nb[0, j] = jnp.zeros((R, UNIT), jnp.bfloat16)

            @pl.when(empty(ahead))
            def _():
                nb[1, j] = jnp.zeros((R, UNIT), jnp.bfloat16)

    @pl.loop(0, NCH)
    def _(i):
        bt[i] = (dot_t(pt_own[...], own_chunk(i)) + dot_t(pt_sib[...], sib[at_chunk(i), :])).astype(jnp.bfloat16)

    def pk_chunk(i):
        return jnp.concatenate([pk[j, at_chunk(i), :] for j in range(U)], axis=1)

    def nb_chunk(j, i):
        return jnp.concatenate([nb[0, j, at_chunk(i), :], nb[1, j, at_chunk(i), :]], axis=1)

    def pair_sums(vt, load, N):
        vacc[:, :N] = jnp.zeros((Wo, N), jnp.float32)

        @pl.loop(0, NCH)
        def _(i):
            vacc[:, :N] += dot(bt[i], load(i))

        for q in range(D):
            vt[q] = vacc[q * S:(q + 1) * S, :N].astype(jnp.bfloat16)

    def reduce(vt, rx, t, sems, N, gap_u, valid):
        parts = []
        for d in range(1, D):
            q, device = peer(d)
            parts.append(remote(vt.at[q], rx.at[d - 1], sems.at[0, d - 1], device))
        for copy in parts:
            copy.start()
        value = vt[me].astype(jnp.float32)
        for d, copy in enumerate(parts):
            copy.wait_recv()
            value = value + rx[d].astype(jnp.float32)
        w = lax.broadcasted_iota(jnp.int32, (S, N), 0) + me * S
        u = lax.broadcasted_iota(jnp.int32, (S, N), 1)
        gap_w = jnp.concatenate([gap_col[me]] * (N // UNIT), axis=1)
        quotient = value / (gap_w + gap_u)
        t[me] = jnp.where(valid(u, w) & (w < total), quotient, 0.0).astype(jnp.bfloat16)
        backs = []
        for d in range(1, D):
            backs.append(remote(t.at[me], t.at[me], sems.at[1, d - 1], peer(d)[1]))
        for copy in backs:
            copy.start()
        for copy in backs:
            copy.wait_recv()
        for copy in parts + backs:
            copy.wait_send()

    pair_sums(vt_o, pk_chunk, W)
    reduce(vt_o, rx_o, t_o, ro_sem, W, gap_row[0:1, :], lambda u, w: u < total)

    @pl.loop(0, NCH)
    def _(i):
        acc[at_chunk(i), :] = dot_t(pk_chunk(i), t_o[...].reshape(Wo, W))

    for copy in gap_copies:
        copy.wait()

    for j in range(U):
        def arrived(side, whole):
            where, end = ((behind, 0), (ahead, n_chip - 1))[side]
            direct, relayed = ((up, relay_down), (down, relay_up))[side]
            there = holds(j, whole, where)

            @pl.when(there & (chip != end) if relay else there)
            def _():
                direct(j, whole).wait_recv()

            if relay:
                @pl.when(there & (chip == end))
                def _():
                    relayed(j, whole).wait_recv()

        for whole in forms(j):
            arrived(0, whole)
            if relay and has(j, edge_halves, whole):
                @pl.when(chip == 1)
                def _():
                    relay_up(j, whole).start()
        for whole in forms(j):
            arrived(1, whole)
            if relay and has(j, edge_halves, whole):
                @pl.when(chip == n_chip - 2)
                def _():
                    relay_down(j, whole).start()
        if False in forms(j):
            for side, where in enumerate((behind, ahead)):
                @pl.when(holds(j, False, where))
                def _():
                    @pl.loop(0, HCH)
                    def _(i):
                        got = nb_half[side, at_chunk(i), :]
                        nb[side, j, at_chunk(i), :] = dot(got, kept).astype(jnp.bfloat16)
                        nb[side, j, at_chunk(i + HCH), :] = dot(got, lowered).astype(jnp.bfloat16)
        pair_sums(vt_u.at[j], lambda i: nb_chunk(j, i), 2 * UNIT)
        cols = slice(j * UNIT, (j + 1) * UNIT)
        gap_u = jnp.concatenate([nb_gap[0, 0:1, cols], nb_gap[1, 0:1, cols]], axis=1)

        def valid(u, w):
            shifted = u + j * UNIT
            from_behind = (shifted < behind_total) & ((shifted >= behind_first) | (w < first))
            place = shifted - UNIT
            from_ahead = (place < ahead_total) & ((place < ahead_first) | (w >= first))
            return ((u < UNIT) & from_behind) | ((u >= UNIT) & from_ahead)

        reduce(vt_u.at[j], rx_u.at[j], t_u.at[j], ru_sem.at[j], 2 * UNIT, gap_u, valid)
        if j < U - 1:
            @pl.loop(0, NCH)
            def _(i):
                acc[at_chunk(i), :] += dot_t(nb_chunk(j, i), t_u[j].reshape(Wo, 2 * UNIT))

    def back(i):
        rows = pl.ds(pl.multiple_of(core * R + i * CH, 16), CH)
        return remote(gsib.at[at_chunk(i), :], out_ref.at[rows, :], f_sem.at[i], sib_id)

    @pl.loop(0, NCH)
    def _(i):
        value = acc[at_chunk(i), :] + dot_t(nb_chunk(U - 1, i), t_u[U - 1].reshape(Wo, 2 * UNIT))
        value = value.astype(jnp.bfloat16)
        gsib[at_chunk(i), :] = dot(value, pt_sib[...]).astype(jnp.bfloat16)
        back(i).start()
        rows = pl.ds(pl.multiple_of(core * R + i * CH, 16), CH)
        out_ref[rows, :] = dot(value, pt_own[...]).astype(jnp.bfloat16)

    @pl.loop(0, NCH)
    def _(i):
        back(i).wait()

    for j in range(U):
        for whole in forms(j):
            @pl.when(sends_up(j, whole))
            def _():
                up(j, whole).wait_send()

            @pl.when(sends_down(j, whole))
            def _():
                down(j, whole).wait_send()

            if relay and has(j, edge_halves, whole):
                @pl.when(chip == 1)
                def _():
                    relay_up(j, whole).wait_send()

                @pl.when(chip == n_chip - 2)
                def _():
                    relay_down(j, whole).wait_send()


def call(n_chip, n_grp, edge_halves, inner_halves, ident, occ_count, aux_count, energy, vir, block):
    U, nv = -(-max(edge_halves, inner_halves) // 2), vir.shape[1]
    rows, C = block.shape
    R = rows // 2
    CH = chunk_rows(R // 2)
    D = 2 * n_grp
    W = U * UNIT
    S = -(-W // (D * 16)) * 16
    Wo = D * S
    N = 2 * UNIT
    dims = (n_chip, n_grp, edge_halves, inner_halves, R, CH, S, D, C, nv)
    bf, f32 = jnp.bfloat16, jnp.float32
    vm, dma = pltpu.VMEM, pltpu.SemaphoreType.DMA
    scratch = [
        vm((8, C), f32), vm((R, C), bf), vm((8, C), f32), vm((C, W), bf), vm((C, W), bf), vm((Wo, C), bf), vm((Wo, C), bf),
        vm((U, R, UNIT), bf), vm((R // 2, UNIT), bf), vm((R // CH, Wo, CH), bf), vm((8, W), f32), vm((D, S, UNIT), f32),
        vm((2, U, R, UNIT), bf), vm((2, R // 2, UNIT), bf), vm((2, 8, W), f32), vm((Wo, W), f32), vm((R, Wo), f32), vm((R, C), bf),
        vm((D, S, W), bf), vm((D, S, W), bf), vm((D, S, W), bf),
        vm((U, D, S, N), bf), vm((U, D, S, N), bf), vm((U, D, S, N), bf),
        dma((2, 2)), dma((2, U, 2)), dma((2, U, 2)), dma((2, 2)), dma((2, D, 2)), dma((U, 2, D, 2)), dma((R // CH, 2)),
    ]
    smem = pl.BlockSpec(memory_space=pltpu.SMEM)
    vmem = pl.BlockSpec(memory_space=pltpu.VMEM)
    return pl.pallas_call(
        functools.partial(kernel, dims),
        out_shape=jax.ShapeDtypeStruct((rows, C), bf),
        in_specs=[smem, smem, smem, vmem, vmem],
        out_specs=vmem,
        scratch_shapes=scratch,
        compiler_params=pltpu.CompilerParams(
            collective_id=ident, has_side_effects=True, vmem_limit_bytes=56 * 1024 * 1024),
        cost_estimate=pl.CostEstimate(flops=12 * R * W * Wo, bytes_accessed=4 * rows * C, transcendentals=0),
    )(occ_count, aux_count, energy, vir, block)


def choose(n_chip, nv, plans, occ_count):
    def kernel(occ_ref, choice_ref):
        def columns(chip):
            return (occ_ref[2 * chip] + occ_ref[2 * chip + 1]) * nv

        edge = jnp.maximum(columns(0), columns(n_chip - 1))
        inner = lax.fori_loop(1, n_chip - 1, lambda i, most: jnp.maximum(most, columns(i)), jnp.int32(0))
        choice = jnp.int32(len(plans) - 1)
        for i in reversed(range(len(plans) - 1)):
            fits = (edge * 2 <= plans[i][0] * UNIT) & (inner * 2 <= plans[i][1] * UNIT)
            choice = jnp.where(fits, jnp.int32(i), choice)
        choice_ref[0] = choice

    smem = pl.BlockSpec(memory_space=pltpu.SMEM)
    found = pl.pallas_call(kernel, out_shape=jax.ShapeDtypeStruct((1,), jnp.int32),
                           in_specs=[smem], out_specs=smem)(occ_count)
    return found[0]


def solution(mesh):
    n_chip, n_grp = mesh.shape["blk"] // 2, mesh.shape["grp"]

    def per_device(three_index, occ_energy, vir_energy, aux_count, occ_count):
        C, nv = three_index.shape[1], vir_energy.shape[0]
        full = 4 * C // UNIT
        if n_chip == 4:
            plans = [(full - 4, full - 3), (full - 3, full - 4), (full - 3, full - 3), (full - 2, full - 4),
                     (full - 4, full - 2), (full - 1, full - 4), (full - 4, full - 1), (full - 2, full - 2),
                     (full, full)]
        else:
            plans = [(full - 3, full - 3), (full - 2, full - 2), (full - 1, full - 1), (full, full)]
        choice = choose(n_chip, nv, plans, occ_count)
        return lax.switch(
            choice,
            [functools.partial(call, n_chip, n_grp, *plan, i + 1) for i, plan in enumerate(plans)],
            occ_count, aux_count, occ_energy, vir_energy.reshape(1, nv), three_index)

    in_specs = (P("grp", "blk"), P("blk"), P(), P(), P())
    return jax.shard_map(
        per_device, mesh=mesh, in_specs=in_specs, out_specs=P("grp", "blk"), check_vma=False)
```

```python
import functools

import jax
import jax.numpy as jnp
from jax import lax
from jax.experimental import pallas as pl
from jax.experimental.pallas import tpu as pltpu
from jax.sharding import PartitionSpec as P

UNIT = 128
last_last = (((1,), (1,)), ((), ()))


def dot(a, b):
    return jnp.dot(a, b, preferred_element_type=jnp.float32)


def dot_t(a, b):
    return lax.dot_general(a, b, last_last, preferred_element_type=jnp.float32)


def chunk_rows(rows):
    return min(c for c in range(16, rows + 1, 16) if rows % c == 0 and c >= min(rows, 192))


def kernel(dims, occ_ref, aux_ref, energy_ref, vir_ref, b_ref, out_ref,
           raw_ref, sib, sib_raw, p_own, p_sib, pt_own, pt_sib, pk, half, bt, gap_row, gap_col,
           nb, nb_half, nb_gap, vacc, acc, gsib,
           vt_o, rx_o, t_o, vt_u, rx_u, t_u,
           x_sem, m_sem, w_sem, g_sem, ro_sem, ru_sem, f_sem):
    n_chip, n_grp, edge_halves, inner_halves, R, CH, S, D, C, nv = dims
    U = -(-max(edge_halves, inner_halves) // 2)
    H = R // 2
    HCH = H // CH
    relay = n_chip == 4
    W = U * UNIT
    Wo = D * S
    NCH = R // CH
    blk = lax.axis_index("blk")
    grp = lax.axis_index("grp")
    chip = blk // 2
    core = blk % 2
    me = grp * 2 + core
    ahead = lax.rem(chip + 1, n_chip)
    behind = lax.rem(chip + n_chip - 1, n_chip)

    def peer(d):
        q = lax.rem(me + d, D)
        return q, {"blk": chip * 2 + q % 2, "grp": q // 2}

    sib_id = {"blk": chip * 2 + 1 - core, "grp": grp}
    ahead_id = {"blk": ahead * 2 + core, "grp": grp}
    behind_id = {"blk": behind * 2 + core, "grp": grp}

    def remote(src, dst, sems, device):
        return pltpu.make_async_remote_copy(
            src_ref=src, dst_ref=dst, send_sem=sems.at[0], recv_sem=sems.at[1],
            device_id=device, device_id_type=pl.DeviceIdType.MESH)

    exact = functools.partial(jnp.dot, precision=lax.Precision.HIGHEST, preferred_element_type=jnp.float32)
    barrier = pltpu.get_barrier_semaphore()
    for d in range(1, D):
        pl.semaphore_signal(barrier, inc=1, device_id=peer(d)[1], device_id_type=pl.DeviceIdType.MESH)
    across_id = {"blk": lax.rem(chip + 2, n_chip) * 2 + core, "grp": grp}
    others = (ahead_id, behind_id) + ((across_id,) if relay else ())
    for device in others:
        pl.semaphore_signal(barrier, inc=1, device_id=device, device_id_type=pl.DeviceIdType.MESH)

    lane = lax.broadcasted_iota(jnp.int32, (8, C), 1)
    spread = jnp.where(lax.broadcasted_iota(jnp.int32, (nv, C), 1) % nv
                       == lax.broadcasted_iota(jnp.int32, (nv, C), 0), 1.0, 0.0)
    gap = -exact(jnp.broadcast_to(vir_ref[...], (8, nv)), spread)
    for k in range(C // nv):
        gap = gap + jnp.where((lane >= k * nv) & (lane < (k + 1) * nv), energy_ref[k], 0.0)
    raw_ref[...] = gap
    pl.semaphore_wait(barrier, D - 1 + len(others))

    other_half = pl.multiple_of((1 - core) * R, 16)
    my_half = pl.multiple_of(core * R, 16)
    swap = remote(b_ref.at[pl.ds(other_half, R), :], sib, x_sem.at[0], sib_id)
    swap_raw = remote(raw_ref, sib_raw, x_sem.at[1], sib_id)
    swap.start()
    swap_raw.start()

    first = occ_ref[chip * 2] * nv
    total = first + occ_ref[chip * 2 + 1] * nv
    ahead_first = occ_ref[ahead * 2] * nv
    ahead_total = ahead_first + occ_ref[ahead * 2 + 1] * nv
    behind_first = occ_ref[behind * 2] * nv
    behind_total = behind_first + occ_ref[behind * 2 + 1] * nv
    own_base, sib_base = core * first, (1 - core) * first
    own_count = core * (total - first) + (1 - core) * first
    sib_count = total - own_count

    def one_hot(shape, col_dim, base, count):
        i = lax.broadcasted_iota(jnp.int32, shape, col_dim)
        j = lax.broadcasted_iota(jnp.int32, shape, 1 - col_dim)
        return jnp.where((i + base == j) & (i < count), 1.0, 0.0)

    p_own[...] = one_hot((C, W), 0, own_base, own_count).astype(jnp.bfloat16)
    p_sib[...] = one_hot((C, W), 0, sib_base, sib_count).astype(jnp.bfloat16)
    pt_own[...] = one_hot((Wo, C), 1, own_base, own_count).astype(jnp.bfloat16)
    pt_sib[...] = one_hot((Wo, C), 1, sib_base, sib_count).astype(jnp.bfloat16)

    swap_raw.wait()
    def three_parts(value):
        high = value.astype(jnp.bfloat16)
        rest = value - high.astype(jnp.float32)
        mid = rest.astype(jnp.bfloat16)
        low = (rest - mid.astype(jnp.float32)).astype(jnp.bfloat16)
        return jnp.concatenate([part.astype(jnp.float32) for part in (high, mid, low)], axis=0).astype(jnp.bfloat16)

    own_parts, sib_parts = three_parts(raw_ref[...]), three_parts(sib_raw[...])
    row = dot(own_parts, p_own[...]) + dot(sib_parts, p_sib[...])
    gap_row[...] = row[0:8] + row[8:16] + row[16:24]
    column = dot_t(pt_own[...], own_parts) + dot_t(pt_sib[...], sib_parts)
    column = column[:, 0:1] + column[:, 8:9] + column[:, 16:17]
    column = jnp.broadcast_to(column, (Wo, UNIT))
    for q in range(D):
        gap_col[q] = column[q * S:(q + 1) * S]
    gap_copies = [remote(gap_row, nb_gap.at[0], g_sem.at[0], ahead_id),
                  remote(gap_row, nb_gap.at[1], g_sem.at[1], behind_id)]
    for copy in gap_copies:
        copy.start()

    aux = aux_ref[grp]
    swap.wait()

    def up(j, whole):
        src, dst = (pk.at[j], nb.at[0, j]) if whole else (half, nb_half.at[0])
        return remote(src, dst, m_sem.at[0, j], ahead_id)

    def down(j, whole):
        src, dst = (pk.at[j], nb.at[1, j]) if whole else (half, nb_half.at[1])
        return remote(src, dst, m_sem.at[1, j], behind_id)

    def relay_up(j, whole):
        src, dst = (nb.at[0, j], nb.at[1, j]) if whole else (nb_half.at[0], nb_half.at[1])
        return remote(src, dst, w_sem.at[0, j], across_id)

    def relay_down(j, whole):
        src, dst = (nb.at[1, j], nb.at[0, j]) if whole else (nb_half.at[1], nb_half.at[0])
        return remote(src, dst, w_sem.at[1, j], across_id)

    def has(j, halves, whole):
        return 2 * j + 2 <= halves if whole else 2 * j + 1 == halves

    def forms(j):
        return [w for w in (True, False) if has(j, edge_halves, w) or has(j, inner_halves, w)]

    def holds(j, whole, where):
        at_end = (where == 0) | (where == n_chip - 1)
        return (has(j, edge_halves, whole) & at_end) | (has(j, inner_halves, whole) & jnp.logical_not(at_end))

    def sends_up(j, whole):
        return holds(j, whole, chip) & (chip != n_chip - 1) if relay else holds(j, whole, chip)

    def sends_down(j, whole):
        return holds(j, whole, chip) & (chip != 0) if relay else holds(j, whole, chip)

    def at_chunk(i):
        return pl.ds(pl.multiple_of(i * CH, 16), CH)

    def own_chunk(i):
        return b_ref[pl.ds(pl.multiple_of(core * R + i * CH, 16), CH), :]

    def masked(i, value):
        row = lax.broadcasted_iota(jnp.int32, (CH, UNIT), 0) + (core * R + i * CH)
        return jnp.where(row < aux, value, 0.0)

    def packed(i, j):
        cols = slice(j * UNIT, (j + 1) * UNIT)
        return masked(i, dot(own_chunk(i), p_own[:, cols]) + dot(sib[at_chunk(i), :], p_sib[:, cols]))

    src_lane = lax.broadcasted_iota(jnp.int32, (UNIT, UNIT), 0)
    dst_lane = lax.broadcasted_iota(jnp.int32, (UNIT, UNIT), 1)
    low = dst_lane < UNIT // 2
    raised = jnp.where(src_lane == dst_lane - UNIT // 2, 1.0, 0.0).astype(jnp.bfloat16)
    kept = jnp.where((src_lane == dst_lane) & low, 1.0, 0.0).astype(jnp.bfloat16)
    lowered = jnp.where(src_lane == dst_lane + UNIT // 2, 1.0, 0.0).astype(jnp.bfloat16)

    end_chip = (chip == 0) | (chip == n_chip - 1)

    def start(j, now):
        for whole in forms(j) if j < U else ():
            @pl.when(sends_up(j, whole) & now)
            def _():
                up(j, whole).start()

            @pl.when(sends_down(j, whole) & now)
            def _():
                down(j, whole).start()

    for j in range(U):
        @pl.loop(0, NCH)
        def _(i):
            pk[j, at_chunk(i), :] = packed(i, j).astype(jnp.bfloat16)

        if False in forms(j):
            @pl.when(holds(j, False, chip))
            def _():
                @pl.loop(0, HCH)
                def _(i):
                    upper = dot(pk[j, at_chunk(i), :], kept)
                    lower = dot(pk[j, at_chunk(i + HCH), :], raised)
                    half[at_chunk(i), :] = (upper + lower).astype(jnp.bfloat16)

        if j == 0 or not relay:
            start(j, True)
        elif j == 1:
            start(j, jnp.logical_not(end_chip))

        def empty(where):
            return jnp.logical_not(holds(j, True, where) | holds(j, False, where))

        if 2 * j >= min(edge_halves, inner_halves):
            @pl.when(empty(behind))
            def _():
                nb[0, j] = jnp.zeros((R, UNIT), jnp.bfloat16)

            @pl.when(empty(ahead))
            def _():
                nb[1, j] = jnp.zeros((R, UNIT), jnp.bfloat16)

    @pl.loop(0, NCH)
    def _(i):
        bt[i] = (dot_t(pt_own[...], own_chunk(i)) + dot_t(pt_sib[...], sib[at_chunk(i), :])).astype(jnp.bfloat16)

    def pk_chunk(i):
        return jnp.concatenate([pk[j, at_chunk(i), :] for j in range(U)], axis=1)

    def nb_chunk(j, i):
        return jnp.concatenate([nb[0, j, at_chunk(i), :], nb[1, j, at_chunk(i), :]], axis=1)

    def pair_sums(vt, load, N):
        vacc[:, :N] = jnp.zeros((Wo, N), jnp.float32)

        @pl.loop(0, NCH)
        def _(i):
            vacc[:, :N] += dot(bt[i], load(i))

        for q in range(D):
            vt[q] = vacc[q * S:(q + 1) * S, :N].astype(jnp.bfloat16)

    def reduce(vt, rx, t, sems, N, gap_u, valid):
        parts = []
        for d in range(1, D):
            q, device = peer(d)
            parts.append(remote(vt.at[q], rx.at[d - 1], sems.at[0, d - 1], device))
        for copy in parts:
            copy.start()
        value = vt[me].astype(jnp.float32)
        for d, copy in enumerate(parts):
            copy.wait_recv()
            value = value + rx[d].astype(jnp.float32)
        w = lax.broadcasted_iota(jnp.int32, (S, N), 0) + me * S
        u = lax.broadcasted_iota(jnp.int32, (S, N), 1)
        gap_w = jnp.concatenate([gap_col[me]] * (N // UNIT), axis=1)
        quotient = value / (gap_w + gap_u)
        t[me] = jnp.where(valid(u, w) & (w < total), quotient, 0.0).astype(jnp.bfloat16)
        backs = []
        for d in range(1, D):
            backs.append(remote(t.at[me], t.at[me], sems.at[1, d - 1], peer(d)[1]))
        for copy in backs:
            copy.start()
        for copy in backs:
            copy.wait_recv()
        for copy in parts + backs:
            copy.wait_send()

    pair_sums(vt_o, pk_chunk, W)
    if relay and U > 1:
        start(1, end_chip)
    reduce(vt_o, rx_o, t_o, ro_sem, W, gap_row[0:1, :], lambda u, w: u < total)

    @pl.loop(0, NCH)
    def _(i):
        acc[at_chunk(i), :] = dot_t(pk_chunk(i), t_o[...].reshape(Wo, W))

    for copy in gap_copies:
        copy.wait()

    for j in range(U):
        def arrived(side, whole, now):
            where, end = ((behind, 0), (ahead, n_chip - 1))[side]
            direct, relayed = ((up, relay_down), (down, relay_up))[side]
            there = holds(j, whole, where) & now

            @pl.when(there & (chip != end) if relay else there)
            def _():
                direct(j, whole).wait_recv()

            if relay:
                @pl.when(there & (chip == end))
                def _():
                    relayed(j, whole).wait_recv()

        odd = chip % 2 == 1 if relay else True
        for whole in forms(j):
            arrived(0, whole, odd)
            if relay and has(j, edge_halves, whole):
                @pl.when(chip == 1)
                def _():
                    relay_up(j, whole).start()
        if relay:
            start(j + 2, odd)
        for whole in forms(j):
            arrived(1, whole, True)
            if relay and has(j, edge_halves, whole):
                @pl.when(chip == n_chip - 2)
                def _():
                    relay_down(j, whole).start()
        if relay:
            start(j + 2, jnp.logical_not(odd))
            for whole in forms(j):
                arrived(0, whole, jnp.logical_not(odd))
        if False in forms(j):
            for side, where in enumerate((behind, ahead)):
                @pl.when(holds(j, False, where))
                def _():
                    @pl.loop(0, HCH)
                    def _(i):
                        got = nb_half[side, at_chunk(i), :]
                        nb[side, j, at_chunk(i), :] = dot(got, kept).astype(jnp.bfloat16)
                        nb[side, j, at_chunk(i + HCH), :] = dot(got, lowered).astype(jnp.bfloat16)
        pair_sums(vt_u.at[j], lambda i: nb_chunk(j, i), 2 * UNIT)
        cols = slice(j * UNIT, (j + 1) * UNIT)
        gap_u = jnp.concatenate([nb_gap[0, 0:1, cols], nb_gap[1, 0:1, cols]], axis=1)

        def valid(u, w):
            shifted = u + j * UNIT
            from_behind = (shifted < behind_total) & ((shifted >= behind_first) | (w < first))
            place = shifted - UNIT
            from_ahead = (place < ahead_total) & ((place < ahead_first) | (w >= first))
            return ((u < UNIT) & from_behind) | ((u >= UNIT) & from_ahead)

        reduce(vt_u.at[j], rx_u.at[j], t_u.at[j], ru_sem.at[j], 2 * UNIT, gap_u, valid)
        if j < U - 1:
            @pl.loop(0, NCH)
            def _(i):
                acc[at_chunk(i), :] += dot_t(nb_chunk(j, i), t_u[j].reshape(Wo, 2 * UNIT))

    def back(i):
        rows = pl.ds(pl.multiple_of(core * R + i * CH, 16), CH)
        return remote(gsib.at[at_chunk(i), :], out_ref.at[rows, :], f_sem.at[i], sib_id)

    @pl.loop(0, NCH)
    def _(i):
        value = acc[at_chunk(i), :] + dot_t(nb_chunk(U - 1, i), t_u[U - 1].reshape(Wo, 2 * UNIT))
        value = value.astype(jnp.bfloat16)
        gsib[at_chunk(i), :] = dot(value, pt_sib[...]).astype(jnp.bfloat16)
        back(i).start()
        rows = pl.ds(pl.multiple_of(core * R + i * CH, 16), CH)
        out_ref[rows, :] = dot(value, pt_own[...]).astype(jnp.bfloat16)

    @pl.loop(0, NCH)
    def _(i):
        back(i).wait()

    for j in range(U):
        for whole in forms(j):
            @pl.when(sends_up(j, whole))
            def _():
                up(j, whole).wait_send()

            @pl.when(sends_down(j, whole))
            def _():
                down(j, whole).wait_send()

            if relay and has(j, edge_halves, whole):
                @pl.when(chip == 1)
                def _():
                    relay_up(j, whole).wait_send()

                @pl.when(chip == n_chip - 2)
                def _():
                    relay_down(j, whole).wait_send()


def call(n_chip, n_grp, edge_halves, inner_halves, ident, occ_count, aux_count, energy, vir, block):
    U, nv = -(-max(edge_halves, inner_halves) // 2), vir.shape[1]
    rows, C = block.shape
    R = rows // 2
    CH = chunk_rows(R // 2)
    D = 2 * n_grp
    W = U * UNIT
    S = -(-W // (D * 16)) * 16
    Wo = D * S
    N = 2 * UNIT
    dims = (n_chip, n_grp, edge_halves, inner_halves, R, CH, S, D, C, nv)
    bf, f32 = jnp.bfloat16, jnp.float32
    vm, dma = pltpu.VMEM, pltpu.SemaphoreType.DMA
    scratch = [
        vm((8, C), f32), vm((R, C), bf), vm((8, C), f32), vm((C, W), bf), vm((C, W), bf), vm((Wo, C), bf), vm((Wo, C), bf),
        vm((U, R, UNIT), bf), vm((R // 2, UNIT), bf), vm((R // CH, Wo, CH), bf), vm((8, W), f32), vm((D, S, UNIT), f32),
        vm((2, U, R, UNIT), bf), vm((2, R // 2, UNIT), bf), vm((2, 8, W), f32), vm((Wo, W), f32), vm((R, Wo), f32), vm((R, C), bf),
        vm((D, S, W), bf), vm((D, S, W), bf), vm((D, S, W), bf),
        vm((U, D, S, N), bf), vm((U, D, S, N), bf), vm((U, D, S, N), bf),
        dma((2, 2)), dma((2, U, 2)), dma((2, U, 2)), dma((2, 2)), dma((2, D, 2)), dma((U, 2, D, 2)), dma((R // CH, 2)),
    ]
    smem = pl.BlockSpec(memory_space=pltpu.SMEM)
    vmem = pl.BlockSpec(memory_space=pltpu.VMEM)
    return pl.pallas_call(
        functools.partial(kernel, dims),
        out_shape=jax.ShapeDtypeStruct((rows, C), bf),
        in_specs=[smem, smem, smem, vmem, vmem],
        out_specs=vmem,
        scratch_shapes=scratch,
        compiler_params=pltpu.CompilerParams(
            collective_id=ident, has_side_effects=True, vmem_limit_bytes=56 * 1024 * 1024),
        cost_estimate=pl.CostEstimate(flops=12 * R * W * Wo, bytes_accessed=4 * rows * C, transcendentals=0),
    )(occ_count, aux_count, energy, vir, block)


def choose(n_chip, nv, plans, occ_count):
    def kernel(occ_ref, choice_ref):
        def columns(chip):
            return (occ_ref[2 * chip] + occ_ref[2 * chip + 1]) * nv

        edge = jnp.maximum(columns(0), columns(n_chip - 1))
        inner = lax.fori_loop(1, n_chip - 1, lambda i, most: jnp.maximum(most, columns(i)), jnp.int32(0))
        choice = jnp.int32(len(plans) - 1)
        for i in reversed(range(len(plans) - 1)):
            fits = (edge * 2 <= plans[i][0] * UNIT) & (inner * 2 <= plans[i][1] * UNIT)
            choice = jnp.where(fits, jnp.int32(i), choice)
        choice_ref[0] = choice

    smem = pl.BlockSpec(memory_space=pltpu.SMEM)
    found = pl.pallas_call(kernel, out_shape=jax.ShapeDtypeStruct((1,), jnp.int32),
                           in_specs=[smem], out_specs=smem)(occ_count)
    return found[0]


def solution(mesh):
    n_chip, n_grp = mesh.shape["blk"] // 2, mesh.shape["grp"]

    def per_device(three_index, occ_energy, vir_energy, aux_count, occ_count):
        C, nv = three_index.shape[1], vir_energy.shape[0]
        full = 4 * C // UNIT
        if n_chip == 4:
            plans = [(full - 3, full - 3), (full - 2, full - 4), (full - 4, full - 2),
                     (full - 1, full - 3), (full - 3, full - 1), (full, full)]
        else:
            plans = [(full - 3, full - 3), (full - 2, full - 2), (full - 1, full - 1), (full, full)]
        choice = choose(n_chip, nv, plans, occ_count)
        return lax.switch(
            choice,
            [functools.partial(call, n_chip, n_grp, *plan, i + 1) for i, plan in enumerate(plans)],
            occ_count, aux_count, occ_energy, vir_energy.reshape(1, nv), three_index)

    in_specs = (P("grp", "blk"), P("blk"), P(), P(), P())
    return jax.shard_map(
        per_device, mesh=mesh, in_specs=in_specs, out_specs=P("grp", "blk"), check_vma=False)
```

```python
import functools

import jax
import jax.numpy as jnp
from jax import lax
from jax.experimental import pallas as pl
from jax.experimental.pallas import tpu as pltpu
from jax.sharding import PartitionSpec as P

UNIT = 128
last_last = (((1,), (1,)), ((), ()))


def dot(a, b):
    return jnp.dot(a, b, preferred_element_type=jnp.float32)


def dot_t(a, b):
    return lax.dot_general(a, b, last_last, preferred_element_type=jnp.float32)


def chunk_rows(rows):
    return min(c for c in range(16, rows + 1, 16) if rows % c == 0 and c >= min(rows, 192))


def kernel(dims, occ_ref, aux_ref, energy_ref, vir_ref, b_ref, out_ref,
           raw_ref, sib, sib_raw, p_own, p_sib, pt_own, pt_sib, pk, half, bt, gap_row, gap_col,
           nb, nb_half, nb_gap, vacc, acc, gsib,
           vt_o, rx_o, t_o, vt_u, rx_u, t_u,
           x_sem, m_sem, w_sem, g_sem, ro_sem, ru_sem, f_sem):
    n_chip, n_grp, edge_halves, inner_halves, R, CH, S, D, C, nv = dims
    U = -(-max(edge_halves, inner_halves) // 2)
    H = R // 2
    HCH = H // CH
    relay = n_chip == 4 and edge_halves > inner_halves
    later = n_chip == 4 and not relay
    W = U * UNIT
    Wo = D * S
    NCH = R // CH
    blk = lax.axis_index("blk")
    grp = lax.axis_index("grp")
    chip = blk // 2
    core = blk % 2
    me = grp * 2 + core
    ahead = lax.rem(chip + 1, n_chip)
    behind = lax.rem(chip + n_chip - 1, n_chip)

    def peer(d):
        q = lax.rem(me + d, D)
        return q, {"blk": chip * 2 + q % 2, "grp": q // 2}

    sib_id = {"blk": chip * 2 + 1 - core, "grp": grp}
    ahead_id = {"blk": ahead * 2 + core, "grp": grp}
    behind_id = {"blk": behind * 2 + core, "grp": grp}

    def remote(src, dst, sems, device):
        return pltpu.make_async_remote_copy(
            src_ref=src, dst_ref=dst, send_sem=sems.at[0], recv_sem=sems.at[1],
            device_id=device, device_id_type=pl.DeviceIdType.MESH)

    exact = functools.partial(jnp.dot, precision=lax.Precision.HIGHEST, preferred_element_type=jnp.float32)
    barrier = pltpu.get_barrier_semaphore()
    for d in range(1, D):
        pl.semaphore_signal(barrier, inc=1, device_id=peer(d)[1], device_id_type=pl.DeviceIdType.MESH)
    across_id = {"blk": lax.rem(chip + 2, n_chip) * 2 + core, "grp": grp}
    others = (ahead_id, behind_id) + ((across_id,) if relay else ())
    for device in others:
        pl.semaphore_signal(barrier, inc=1, device_id=device, device_id_type=pl.DeviceIdType.MESH)

    lane = lax.broadcasted_iota(jnp.int32, (8, C), 1)
    spread = jnp.where(lax.broadcasted_iota(jnp.int32, (nv, C), 1) % nv
                       == lax.broadcasted_iota(jnp.int32, (nv, C), 0), 1.0, 0.0)
    gap = -exact(jnp.broadcast_to(vir_ref[...], (8, nv)), spread)
    for k in range(C // nv):
        gap = gap + jnp.where((lane >= k * nv) & (lane < (k + 1) * nv), energy_ref[k], 0.0)
    raw_ref[...] = gap
    pl.semaphore_wait(barrier, D - 1 + len(others))

    other_half = pl.multiple_of((1 - core) * R, 16)
    my_half = pl.multiple_of(core * R, 16)
    swap = remote(b_ref.at[pl.ds(other_half, R), :], sib, x_sem.at[0], sib_id)
    swap_raw = remote(raw_ref, sib_raw, x_sem.at[1], sib_id)
    swap.start()
    swap_raw.start()

    first = occ_ref[chip * 2] * nv
    total = first + occ_ref[chip * 2 + 1] * nv
    ahead_first = occ_ref[ahead * 2] * nv
    ahead_total = ahead_first + occ_ref[ahead * 2 + 1] * nv
    behind_first = occ_ref[behind * 2] * nv
    behind_total = behind_first + occ_ref[behind * 2 + 1] * nv
    own_base, sib_base = core * first, (1 - core) * first
    own_count = core * (total - first) + (1 - core) * first
    sib_count = total - own_count

    def one_hot(shape, col_dim, base, count):
        i = lax.broadcasted_iota(jnp.int32, shape, col_dim)
        j = lax.broadcasted_iota(jnp.int32, shape, 1 - col_dim)
        return jnp.where((i + base == j) & (i < count), 1.0, 0.0)

    p_own[...] = one_hot((C, W), 0, own_base, own_count).astype(jnp.bfloat16)
    p_sib[...] = one_hot((C, W), 0, sib_base, sib_count).astype(jnp.bfloat16)
    pt_own[...] = one_hot((Wo, C), 1, own_base, own_count).astype(jnp.bfloat16)
    pt_sib[...] = one_hot((Wo, C), 1, sib_base, sib_count).astype(jnp.bfloat16)

    swap_raw.wait()
    def three_parts(value):
        high = value.astype(jnp.bfloat16)
        rest = value - high.astype(jnp.float32)
        mid = rest.astype(jnp.bfloat16)
        low = (rest - mid.astype(jnp.float32)).astype(jnp.bfloat16)
        return jnp.concatenate([part.astype(jnp.float32) for part in (high, mid, low)], axis=0).astype(jnp.bfloat16)

    own_parts, sib_parts = three_parts(raw_ref[...]), three_parts(sib_raw[...])
    row = dot(own_parts, p_own[...]) + dot(sib_parts, p_sib[...])
    gap_row[...] = row[0:8] + row[8:16] + row[16:24]
    column = dot_t(pt_own[...], own_parts) + dot_t(pt_sib[...], sib_parts)
    column = column[:, 0:1] + column[:, 8:9] + column[:, 16:17]
    column = jnp.broadcast_to(column, (Wo, UNIT))
    for q in range(D):
        gap_col[q] = column[q * S:(q + 1) * S]
    gap_copies = [remote(gap_row, nb_gap.at[0], g_sem.at[0], ahead_id),
                  remote(gap_row, nb_gap.at[1], g_sem.at[1], behind_id)]
    for copy in gap_copies:
        copy.start()

    aux = aux_ref[grp]
    swap.wait()

    def up(j, whole):
        src, dst = (pk.at[j], nb.at[0, j]) if whole else (half, nb_half.at[0])
        return remote(src, dst, m_sem.at[0, j], ahead_id)

    def down(j, whole):
        src, dst = (pk.at[j], nb.at[1, j]) if whole else (half, nb_half.at[1])
        return remote(src, dst, m_sem.at[1, j], behind_id)

    def relay_up(j, whole):
        src, dst = (nb.at[0, j], nb.at[1, j]) if whole else (nb_half.at[0], nb_half.at[1])
        return remote(src, dst, w_sem.at[0, j], across_id)

    def relay_down(j, whole):
        src, dst = (nb.at[1, j], nb.at[0, j]) if whole else (nb_half.at[1], nb_half.at[0])
        return remote(src, dst, w_sem.at[1, j], across_id)

    def has(j, halves, whole):
        return 2 * j + 2 <= halves if whole else 2 * j + 1 == halves

    def forms(j):
        return [w for w in (True, False) if has(j, edge_halves, w) or has(j, inner_halves, w)]

    def holds(j, whole, where):
        at_end = (where == 0) | (where == n_chip - 1)
        return (has(j, edge_halves, whole) & at_end) | (has(j, inner_halves, whole) & jnp.logical_not(at_end))

    def sends_up(j, whole):
        return holds(j, whole, chip) & (chip != n_chip - 1) if relay else holds(j, whole, chip)

    def sends_down(j, whole):
        return holds(j, whole, chip) & (chip != 0) if relay else holds(j, whole, chip)

    def at_chunk(i):
        return pl.ds(pl.multiple_of(i * CH, 16), CH)

    def own_chunk(i):
        return b_ref[pl.ds(pl.multiple_of(core * R + i * CH, 16), CH), :]

    def masked(i, value):
        row = lax.broadcasted_iota(jnp.int32, (CH, UNIT), 0) + (core * R + i * CH)
        return jnp.where(row < aux, value, 0.0)

    def packed(i, j):
        cols = slice(j * UNIT, (j + 1) * UNIT)
        return masked(i, dot(own_chunk(i), p_own[:, cols]) + dot(sib[at_chunk(i), :], p_sib[:, cols]))

    src_lane = lax.broadcasted_iota(jnp.int32, (UNIT, UNIT), 0)
    dst_lane = lax.broadcasted_iota(jnp.int32, (UNIT, UNIT), 1)
    low = dst_lane < UNIT // 2
    raised = jnp.where(src_lane == dst_lane - UNIT // 2, 1.0, 0.0).astype(jnp.bfloat16)
    kept = jnp.where((src_lane == dst_lane) & low, 1.0, 0.0).astype(jnp.bfloat16)
    lowered = jnp.where(src_lane == dst_lane + UNIT // 2, 1.0, 0.0).astype(jnp.bfloat16)

    def start(j, now_up, now_down):
        for whole in forms(j):
            @pl.when(sends_up(j, whole) & now_up)
            def _():
                up(j, whole).start()

            @pl.when(sends_down(j, whole) & now_down)
            def _():
                down(j, whole).start()

    for j in range(U):
        @pl.loop(0, NCH)
        def _(i):
            pk[j, at_chunk(i), :] = packed(i, j).astype(jnp.bfloat16)

        if False in forms(j):
            @pl.when(holds(j, False, chip))
            def _():
                @pl.loop(0, HCH)
                def _(i):
                    upper = dot(pk[j, at_chunk(i), :], kept)
                    lower = dot(pk[j, at_chunk(i + HCH), :], raised)
                    half[at_chunk(i), :] = (upper + lower).astype(jnp.bfloat16)

        start(j, chip != n_chip - 1 if later else True, chip != 0 if later else True)

        def empty(where):
            return jnp.logical_not(holds(j, True, where) | holds(j, False, where))

        if 2 * j >= min(edge_halves, inner_halves):
            @pl.when(empty(behind))
            def _():
                nb[0, j] = jnp.zeros((R, UNIT), jnp.bfloat16)

            @pl.when(empty(ahead))
            def _():
                nb[1, j] = jnp.zeros((R, UNIT), jnp.bfloat16)

    @pl.loop(0, NCH)
    def _(i):
        bt[i] = (dot_t(pt_own[...], own_chunk(i)) + dot_t(pt_sib[...], sib[at_chunk(i), :])).astype(jnp.bfloat16)

    def pk_chunk(i):
        return jnp.concatenate([pk[j, at_chunk(i), :] for j in range(U)], axis=1)

    def nb_chunk(j, i):
        return jnp.concatenate([nb[0, j, at_chunk(i), :], nb[1, j, at_chunk(i), :]], axis=1)

    def pair_sums(vt, load, N):
        vacc[:, :N] = jnp.zeros((Wo, N), jnp.float32)

        @pl.loop(0, NCH)
        def _(i):
            vacc[:, :N] += dot(bt[i], load(i))

        for q in range(D):
            vt[q] = vacc[q * S:(q + 1) * S, :N].astype(jnp.bfloat16)

    def reduce(vt, rx, t, sems, N, gap_u, valid):
        parts = []
        for d in range(1, D):
            q, device = peer(d)
            parts.append(remote(vt.at[q], rx.at[d - 1], sems.at[0, d - 1], device))
        for copy in parts:
            copy.start()
        value = vt[me].astype(jnp.float32)
        for d, copy in enumerate(parts):
            copy.wait_recv()
            value = value + rx[d].astype(jnp.float32)
        w = lax.broadcasted_iota(jnp.int32, (S, N), 0) + me * S
        u = lax.broadcasted_iota(jnp.int32, (S, N), 1)
        gap_w = jnp.concatenate([gap_col[me]] * (N // UNIT), axis=1)
        quotient = value / (gap_w + gap_u)
        t[me] = jnp.where(valid(u, w) & (w < total), quotient, 0.0).astype(jnp.bfloat16)
        backs = []
        for d in range(1, D):
            backs.append(remote(t.at[me], t.at[me], sems.at[1, d - 1], peer(d)[1]))
        for copy in backs:
            copy.start()
        for copy in backs:
            copy.wait_recv()
        for copy in parts + backs:
            copy.wait_send()

    pair_sums(vt_o, pk_chunk, W)
    if later:
        for j in range(U):
            start(j, chip == n_chip - 1, chip == 0)
    reduce(vt_o, rx_o, t_o, ro_sem, W, gap_row[0:1, :], lambda u, w: u < total)

    @pl.loop(0, NCH)
    def _(i):
        acc[at_chunk(i), :] = dot_t(pk_chunk(i), t_o[...].reshape(Wo, W))

    for copy in gap_copies:
        copy.wait()

    for j in range(U):
        def arrived(side, whole, now):
            where, end = ((behind, 0), (ahead, n_chip - 1))[side]
            direct, relayed = ((up, relay_down), (down, relay_up))[side]
            there = holds(j, whole, where) & now

            @pl.when(there & (chip != end) if relay else there)
            def _():
                direct(j, whole).wait_recv()

            if relay:
                @pl.when(there & (chip == end))
                def _():
                    relayed(j, whole).wait_recv()

        odd = chip % 2 == 1 if relay else True
        for whole in forms(j):
            arrived(0, whole, odd)
            if relay and has(j, edge_halves, whole):
                @pl.when(chip == 1)
                def _():
                    relay_up(j, whole).start()
        for whole in forms(j):
            arrived(1, whole, True)
            if relay and has(j, edge_halves, whole):
                @pl.when(chip == n_chip - 2)
                def _():
                    relay_down(j, whole).start()
        if relay:
            for whole in forms(j):
                arrived(0, whole, jnp.logical_not(odd))
        if False in forms(j):
            for side, where in enumerate((behind, ahead)):
                @pl.when(holds(j, False, where))
                def _():
                    @pl.loop(0, HCH)
                    def _(i):
                        got = nb_half[side, at_chunk(i), :]
                        nb[side, j, at_chunk(i), :] = dot(got, kept).astype(jnp.bfloat16)
                        nb[side, j, at_chunk(i + HCH), :] = dot(got, lowered).astype(jnp.bfloat16)
        pair_sums(vt_u.at[j], lambda i: nb_chunk(j, i), 2 * UNIT)
        cols = slice(j * UNIT, (j + 1) * UNIT)
        gap_u = jnp.concatenate([nb_gap[0, 0:1, cols], nb_gap[1, 0:1, cols]], axis=1)

        def valid(u, w):
            shifted = u + j * UNIT
            from_behind = (shifted < behind_total) & ((shifted >= behind_first) | (w < first))
            place = shifted - UNIT
            from_ahead = (place < ahead_total) & ((place < ahead_first) | (w >= first))
            return ((u < UNIT) & from_behind) | ((u >= UNIT) & from_ahead)

        reduce(vt_u.at[j], rx_u.at[j], t_u.at[j], ru_sem.at[j], 2 * UNIT, gap_u, valid)
        if j < U - 1:
            @pl.loop(0, NCH)
            def _(i):
                acc[at_chunk(i), :] += dot_t(nb_chunk(j, i), t_u[j].reshape(Wo, 2 * UNIT))

    def back(i):
        rows = pl.ds(pl.multiple_of(core * R + i * CH, 16), CH)
        return remote(gsib.at[at_chunk(i), :], out_ref.at[rows, :], f_sem.at[i], sib_id)

    @pl.loop(0, NCH)
    def _(i):
        value = acc[at_chunk(i), :] + dot_t(nb_chunk(U - 1, i), t_u[U - 1].reshape(Wo, 2 * UNIT))
        value = value.astype(jnp.bfloat16)
        gsib[at_chunk(i), :] = dot(value, pt_sib[...]).astype(jnp.bfloat16)
        back(i).start()
        rows = pl.ds(pl.multiple_of(core * R + i * CH, 16), CH)
        out_ref[rows, :] = dot(value, pt_own[...]).astype(jnp.bfloat16)

    @pl.loop(0, NCH)
    def _(i):
        back(i).wait()

    for j in range(U):
        for whole in forms(j):
            @pl.when(sends_up(j, whole))
            def _():
                up(j, whole).wait_send()

            @pl.when(sends_down(j, whole))
            def _():
                down(j, whole).wait_send()

            if relay and has(j, edge_halves, whole):
                @pl.when(chip == 1)
                def _():
                    relay_up(j, whole).wait_send()

                @pl.when(chip == n_chip - 2)
                def _():
                    relay_down(j, whole).wait_send()


def call(n_chip, n_grp, edge_halves, inner_halves, ident, occ_count, aux_count, energy, vir, block):
    U, nv = -(-max(edge_halves, inner_halves) // 2), vir.shape[1]
    rows, C = block.shape
    R = rows // 2
    CH = chunk_rows(R // 2)
    D = 2 * n_grp
    W = U * UNIT
    S = -(-W // (D * 16)) * 16
    Wo = D * S
    N = 2 * UNIT
    dims = (n_chip, n_grp, edge_halves, inner_halves, R, CH, S, D, C, nv)
    bf, f32 = jnp.bfloat16, jnp.float32
    vm, dma = pltpu.VMEM, pltpu.SemaphoreType.DMA
    scratch = [
        vm((8, C), f32), vm((R, C), bf), vm((8, C), f32), vm((C, W), bf), vm((C, W), bf), vm((Wo, C), bf), vm((Wo, C), bf),
        vm((U, R, UNIT), bf), vm((R // 2, UNIT), bf), vm((R // CH, Wo, CH), bf), vm((8, W), f32), vm((D, S, UNIT), f32),
        vm((2, U, R, UNIT), bf), vm((2, R // 2, UNIT), bf), vm((2, 8, W), f32), vm((Wo, W), f32), vm((R, Wo), f32), vm((R, C), bf),
        vm((D, S, W), bf), vm((D, S, W), bf), vm((D, S, W), bf),
        vm((U, D, S, N), bf), vm((U, D, S, N), bf), vm((U, D, S, N), bf),
        dma((2, 2)), dma((2, U, 2)), dma((2, U, 2)), dma((2, 2)), dma((2, D, 2)), dma((U, 2, D, 2)), dma((R // CH, 2)),
    ]
    smem = pl.BlockSpec(memory_space=pltpu.SMEM)
    vmem = pl.BlockSpec(memory_space=pltpu.VMEM)
    return pl.pallas_call(
        functools.partial(kernel, dims),
        out_shape=jax.ShapeDtypeStruct((rows, C), bf),
        in_specs=[smem, smem, smem, vmem, vmem],
        out_specs=vmem,
        scratch_shapes=scratch,
        compiler_params=pltpu.CompilerParams(
            collective_id=ident, has_side_effects=True, vmem_limit_bytes=56 * 1024 * 1024),
        cost_estimate=pl.CostEstimate(flops=12 * R * W * Wo, bytes_accessed=4 * rows * C, transcendentals=0),
    )(occ_count, aux_count, energy, vir, block)


def choose(n_chip, nv, plans, occ_count):
    def kernel(occ_ref, choice_ref):
        def columns(chip):
            return (occ_ref[2 * chip] + occ_ref[2 * chip + 1]) * nv

        edge = jnp.maximum(columns(0), columns(n_chip - 1))
        inner = lax.fori_loop(1, n_chip - 1, lambda i, most: jnp.maximum(most, columns(i)), jnp.int32(0))
        choice = jnp.int32(len(plans) - 1)
        for i in reversed(range(len(plans) - 1)):
            fits = (edge * 2 <= plans[i][0] * UNIT) & (inner * 2 <= plans[i][1] * UNIT)
            choice = jnp.where(fits, jnp.int32(i), choice)
        choice_ref[0] = choice

    smem = pl.BlockSpec(memory_space=pltpu.SMEM)
    found = pl.pallas_call(kernel, out_shape=jax.ShapeDtypeStruct((1,), jnp.int32),
                           in_specs=[smem], out_specs=smem)(occ_count)
    return found[0]


def solution(mesh):
    n_chip, n_grp = mesh.shape["blk"] // 2, mesh.shape["grp"]

    def per_device(three_index, occ_energy, vir_energy, aux_count, occ_count):
        C, nv = three_index.shape[1], vir_energy.shape[0]
        full = 4 * C // UNIT
        if n_chip == 4:
            plans = [(full - 3, full - 3), (full - 2, full - 4), (full - 4, full - 2),
                     (full - 1, full - 3), (full - 3, full - 1), (full, full)]
        else:
            plans = [(full - 3, full - 3), (full - 2, full - 2), (full - 1, full - 1), (full, full)]
        choice = choose(n_chip, nv, plans, occ_count)
        return lax.switch(
            choice,
            [functools.partial(call, n_chip, n_grp, *plan, i + 1) for i, plan in enumerate(plans)],
            occ_count, aux_count, occ_energy, vir_energy.reshape(1, nv), three_index)

    in_specs = (P("grp", "blk"), P("blk"), P(), P(), P())
    return jax.shard_map(
        per_device, mesh=mesh, in_specs=in_specs, out_specs=P("grp", "blk"), check_vma=False)
```

```python
import functools

import jax
import jax.numpy as jnp
from jax import lax
from jax.experimental import pallas as pl
from jax.experimental.pallas import tpu as pltpu
from jax.sharding import PartitionSpec as P

UNIT = 128
last_last = (((1,), (1,)), ((), ()))


def dot(a, b):
    return jnp.dot(a, b, preferred_element_type=jnp.float32)


def dot_t(a, b):
    return lax.dot_general(a, b, last_last, preferred_element_type=jnp.float32)


def chunk_rows(rows):
    return min(c for c in range(16, rows + 1, 16) if rows % c == 0 and c >= min(rows, 192))


def kernel(dims, occ_ref, aux_ref, energy_ref, vir_ref, b_ref, out_ref,
           raw_ref, sib, sib_raw, p_own, p_sib, pt_own, pt_sib, pk, half, bt, gap_row, gap_col,
           nb, nb_half, nb_gap, vacc, acc, gsib,
           vt_o, rx_o, t_o, vt_u, rx_u, t_u,
           x_sem, m_sem, w_sem, g_sem, ro_sem, ru_sem, f_sem):
    n_chip, n_grp, edge_halves, inner_halves, R, CH, S, D, C, nv = dims
    U = -(-max(edge_halves, inner_halves) // 2)
    H = R // 2
    HCH = H // CH
    relay = n_chip == 4
    W = U * UNIT
    Wo = D * S
    NCH = R // CH
    blk = lax.axis_index("blk")
    grp = lax.axis_index("grp")
    chip = blk // 2
    core = blk % 2
    me = grp * 2 + core
    ahead = lax.rem(chip + 1, n_chip)
    behind = lax.rem(chip + n_chip - 1, n_chip)

    def peer(d):
        q = lax.rem(me + d, D)
        return q, {"blk": chip * 2 + q % 2, "grp": q // 2}

    sib_id = {"blk": chip * 2 + 1 - core, "grp": grp}
    ahead_id = {"blk": ahead * 2 + core, "grp": grp}
    behind_id = {"blk": behind * 2 + core, "grp": grp}

    def remote(src, dst, sems, device):
        return pltpu.make_async_remote_copy(
            src_ref=src, dst_ref=dst, send_sem=sems.at[0], recv_sem=sems.at[1],
            device_id=device, device_id_type=pl.DeviceIdType.MESH)

    exact = functools.partial(jnp.dot, precision=lax.Precision.HIGHEST, preferred_element_type=jnp.float32)
    barrier = pltpu.get_barrier_semaphore()
    for d in range(1, D):
        pl.semaphore_signal(barrier, inc=1, device_id=peer(d)[1], device_id_type=pl.DeviceIdType.MESH)
    across_id = {"blk": lax.rem(chip + 2, n_chip) * 2 + core, "grp": grp}
    others = (ahead_id, behind_id) + ((across_id,) if relay else ())
    for device in others:
        pl.semaphore_signal(barrier, inc=1, device_id=device, device_id_type=pl.DeviceIdType.MESH)

    lane = lax.broadcasted_iota(jnp.int32, (8, C), 1)
    spread = jnp.where(lax.broadcasted_iota(jnp.int32, (nv, C), 1) % nv
                       == lax.broadcasted_iota(jnp.int32, (nv, C), 0), 1.0, 0.0)
    gap = -exact(jnp.broadcast_to(vir_ref[...], (8, nv)), spread)
    for k in range(C // nv):
        gap = gap + jnp.where((lane >= k * nv) & (lane < (k + 1) * nv), energy_ref[k], 0.0)
    raw_ref[...] = gap
    pl.semaphore_wait(barrier, D - 1 + len(others))

    other_half = pl.multiple_of((1 - core) * R, 16)
    my_half = pl.multiple_of(core * R, 16)
    swap = remote(b_ref.at[pl.ds(other_half, R), :], sib, x_sem.at[0], sib_id)
    swap_raw = remote(raw_ref, sib_raw, x_sem.at[1], sib_id)
    swap.start()
    swap_raw.start()

    first = occ_ref[chip * 2] * nv
    total = first + occ_ref[chip * 2 + 1] * nv
    ahead_first = occ_ref[ahead * 2] * nv
    ahead_total = ahead_first + occ_ref[ahead * 2 + 1] * nv
    behind_first = occ_ref[behind * 2] * nv
    behind_total = behind_first + occ_ref[behind * 2 + 1] * nv
    own_base, sib_base = core * first, (1 - core) * first
    own_count = core * (total - first) + (1 - core) * first
    sib_count = total - own_count

    def one_hot(shape, col_dim, base, count):
        i = lax.broadcasted_iota(jnp.int32, shape, col_dim)
        j = lax.broadcasted_iota(jnp.int32, shape, 1 - col_dim)
        return jnp.where((i + base == j) & (i < count), 1.0, 0.0)

    p_own[...] = one_hot((C, W), 0, own_base, own_count).astype(jnp.bfloat16)
    p_sib[...] = one_hot((C, W), 0, sib_base, sib_count).astype(jnp.bfloat16)
    pt_own[...] = one_hot((Wo, C), 1, own_base, own_count).astype(jnp.bfloat16)
    pt_sib[...] = one_hot((Wo, C), 1, sib_base, sib_count).astype(jnp.bfloat16)

    swap_raw.wait()
    def three_parts(value):
        high = value.astype(jnp.bfloat16)
        rest = value - high.astype(jnp.float32)
        mid = rest.astype(jnp.bfloat16)
        low = (rest - mid.astype(jnp.float32)).astype(jnp.bfloat16)
        return jnp.concatenate([part.astype(jnp.float32) for part in (high, mid, low)], axis=0).astype(jnp.bfloat16)

    own_parts, sib_parts = three_parts(raw_ref[...]), three_parts(sib_raw[...])
    row = dot(own_parts, p_own[...]) + dot(sib_parts, p_sib[...])
    gap_row[...] = row[0:8] + row[8:16] + row[16:24]
    column = dot_t(pt_own[...], own_parts) + dot_t(pt_sib[...], sib_parts)
    column = column[:, 0:1] + column[:, 8:9] + column[:, 16:17]
    column = jnp.broadcast_to(column, (Wo, UNIT))
    for q in range(D):
        gap_col[q] = column[q * S:(q + 1) * S]
    gap_copies = [remote(gap_row, nb_gap.at[0], g_sem.at[0], ahead_id),
                  remote(gap_row, nb_gap.at[1], g_sem.at[1], behind_id)]
    for copy in gap_copies:
        copy.start()

    aux = aux_ref[grp]
    swap.wait()

    def up(j, whole):
        src, dst = (pk.at[j], nb.at[0, j]) if whole else (half, nb_half.at[0])
        return remote(src, dst, m_sem.at[0, j], ahead_id)

    def down(j, whole):
        src, dst = (pk.at[j], nb.at[1, j]) if whole else (half, nb_half.at[1])
        return remote(src, dst, m_sem.at[1, j], behind_id)

    def relay_up(j, whole):
        src, dst = (nb.at[0, j], nb.at[1, j]) if whole else (nb_half.at[0], nb_half.at[1])
        return remote(src, dst, w_sem.at[0, j], across_id)

    def relay_down(j, whole):
        src, dst = (nb.at[1, j], nb.at[0, j]) if whole else (nb_half.at[1], nb_half.at[0])
        return remote(src, dst, w_sem.at[1, j], across_id)

    def has(j, halves, whole):
        return 2 * j + 2 <= halves if whole else 2 * j + 1 == halves

    def forms(j):
        return [w for w in (True, False) if has(j, edge_halves, w) or has(j, inner_halves, w)]

    def holds(j, whole, where):
        at_end = (where == 0) | (where == n_chip - 1)
        return (has(j, edge_halves, whole) & at_end) | (has(j, inner_halves, whole) & jnp.logical_not(at_end))

    def sends_up(j, whole):
        return holds(j, whole, chip) & (chip != n_chip - 1) if relay else holds(j, whole, chip)

    def sends_down(j, whole):
        return holds(j, whole, chip) & (chip != 0) if relay else holds(j, whole, chip)

    def at_chunk(i):
        return pl.ds(pl.multiple_of(i * CH, 16), CH)

    def own_chunk(i):
        return b_ref[pl.ds(pl.multiple_of(core * R + i * CH, 16), CH), :]

    def masked(i, value):
        row = lax.broadcasted_iota(jnp.int32, (CH, UNIT), 0) + (core * R + i * CH)
        return jnp.where(row < aux, value, 0.0)

    def packed(i, j):
        cols = slice(j * UNIT, (j + 1) * UNIT)
        return masked(i, dot(own_chunk(i), p_own[:, cols]) + dot(sib[at_chunk(i), :], p_sib[:, cols]))

    src_lane = lax.broadcasted_iota(jnp.int32, (UNIT, UNIT), 0)
    dst_lane = lax.broadcasted_iota(jnp.int32, (UNIT, UNIT), 1)
    low = dst_lane < UNIT // 2
    raised = jnp.where(src_lane == dst_lane - UNIT // 2, 1.0, 0.0).astype(jnp.bfloat16)
    kept = jnp.where((src_lane == dst_lane) & low, 1.0, 0.0).astype(jnp.bfloat16)
    lowered = jnp.where(src_lane == dst_lane + UNIT // 2, 1.0, 0.0).astype(jnp.bfloat16)

    def start(j, now):
        for whole in forms(j) if j < U else ():
            @pl.when(sends_up(j, whole) & now)
            def _():
                up(j, whole).start()

            @pl.when(sends_down(j, whole) & now)
            def _():
                down(j, whole).start()

    for j in range(U):
        @pl.loop(0, NCH)
        def _(i):
            pk[j, at_chunk(i), :] = packed(i, j).astype(jnp.bfloat16)

        if False in forms(j):
            @pl.when(holds(j, False, chip))
            def _():
                @pl.loop(0, HCH)
                def _(i):
                    upper = dot(pk[j, at_chunk(i), :], kept)
                    lower = dot(pk[j, at_chunk(i + HCH), :], raised)
                    half[at_chunk(i), :] = (upper + lower).astype(jnp.bfloat16)

        start(j, True)

        def empty(where):
            return jnp.logical_not(holds(j, True, where) | holds(j, False, where))

        if 2 * j >= min(edge_halves, inner_halves):
            @pl.when(empty(behind))
            def _():
                nb[0, j] = jnp.zeros((R, UNIT), jnp.bfloat16)

            @pl.when(empty(ahead))
            def _():
                nb[1, j] = jnp.zeros((R, UNIT), jnp.bfloat16)

    @pl.loop(0, NCH)
    def _(i):
        bt[i] = (dot_t(pt_own[...], own_chunk(i)) + dot_t(pt_sib[...], sib[at_chunk(i), :])).astype(jnp.bfloat16)

    def pk_chunk(i):
        return jnp.concatenate([pk[j, at_chunk(i), :] for j in range(U)], axis=1)

    def nb_chunk(j, i):
        return jnp.concatenate([nb[0, j, at_chunk(i), :], nb[1, j, at_chunk(i), :]], axis=1)

    def pair_sums(vt, load, N):
        vacc[:, :N] = jnp.zeros((Wo, N), jnp.float32)

        @pl.loop(0, NCH)
        def _(i):
            vacc[:, :N] += dot(bt[i], load(i))

        for q in range(D):
            vt[q] = vacc[q * S:(q + 1) * S, :N].astype(jnp.bfloat16)

    def reduce(vt, rx, t, sems, N, gap_u, valid):
        parts = []
        for d in range(1, D):
            q, device = peer(d)
            parts.append(remote(vt.at[q], rx.at[d - 1], sems.at[0, d - 1], device))
        for copy in parts:
            copy.start()
        value = vt[me].astype(jnp.float32)
        for d, copy in enumerate(parts):
            copy.wait_recv()
            value = value + rx[d].astype(jnp.float32)
        w = lax.broadcasted_iota(jnp.int32, (S, N), 0) + me * S
        u = lax.broadcasted_iota(jnp.int32, (S, N), 1)
        gap_w = jnp.concatenate([gap_col[me]] * (N // UNIT), axis=1)
        quotient = value / (gap_w + gap_u)
        t[me] = jnp.where(valid(u, w) & (w < total), quotient, 0.0).astype(jnp.bfloat16)
        backs = []
        for d in range(1, D):
            backs.append(remote(t.at[me], t.at[me], sems.at[1, d - 1], peer(d)[1]))
        for copy in backs:
            copy.start()
        for copy in backs:
            copy.wait_recv()
        for copy in parts + backs:
            copy.wait_send()

    pair_sums(vt_o, pk_chunk, W)
    reduce(vt_o, rx_o, t_o, ro_sem, W, gap_row[0:1, :], lambda u, w: u < total)

    @pl.loop(0, NCH)
    def _(i):
        acc[at_chunk(i), :] = dot_t(pk_chunk(i), t_o[...].reshape(Wo, W))

    for copy in gap_copies:
        copy.wait()

    for j in range(U):
        def arrived(side, whole, now):
            where, end = ((behind, 0), (ahead, n_chip - 1))[side]
            direct, relayed = ((up, relay_down), (down, relay_up))[side]
            there = holds(j, whole, where) & now

            @pl.when(there & (chip != end) if relay else there)
            def _():
                direct(j, whole).wait_recv()

            if relay:
                @pl.when(there & (chip == end))
                def _():
                    relayed(j, whole).wait_recv()

        odd = chip % 2 == 1 if relay else True
        for whole in forms(j):
            arrived(0, whole, odd)
            if relay and has(j, edge_halves, whole):
                @pl.when(chip == 1)
                def _():
                    relay_up(j, whole).start()
        for whole in forms(j):
            arrived(1, whole, True)
            if relay and has(j, edge_halves, whole):
                @pl.when(chip == n_chip - 2)
                def _():
                    relay_down(j, whole).start()
        if relay:
            for whole in forms(j):
                arrived(0, whole, jnp.logical_not(odd))
        if False in forms(j):
            for side, where in enumerate((behind, ahead)):
                @pl.when(holds(j, False, where))
                def _():
                    @pl.loop(0, HCH)
                    def _(i):
                        got = nb_half[side, at_chunk(i), :]
                        nb[side, j, at_chunk(i), :] = dot(got, kept).astype(jnp.bfloat16)
                        nb[side, j, at_chunk(i + HCH), :] = dot(got, lowered).astype(jnp.bfloat16)
        pair_sums(vt_u.at[j], lambda i: nb_chunk(j, i), 2 * UNIT)
        cols = slice(j * UNIT, (j + 1) * UNIT)
        gap_u = jnp.concatenate([nb_gap[0, 0:1, cols], nb_gap[1, 0:1, cols]], axis=1)

        def valid(u, w):
            shifted = u + j * UNIT
            from_behind = (shifted < behind_total) & ((shifted >= behind_first) | (w < first))
            place = shifted - UNIT
            from_ahead = (place < ahead_total) & ((place < ahead_first) | (w >= first))
            return ((u < UNIT) & from_behind) | ((u >= UNIT) & from_ahead)

        reduce(vt_u.at[j], rx_u.at[j], t_u.at[j], ru_sem.at[j], 2 * UNIT, gap_u, valid)
        if j < U - 1:
            @pl.loop(0, NCH)
            def _(i):
                acc[at_chunk(i), :] += dot_t(nb_chunk(j, i), t_u[j].reshape(Wo, 2 * UNIT))

    def back(i):
        rows = pl.ds(pl.multiple_of(core * R + i * CH, 16), CH)
        return remote(gsib.at[at_chunk(i), :], out_ref.at[rows, :], f_sem.at[i], sib_id)

    @pl.loop(0, NCH)
    def _(i):
        value = acc[at_chunk(i), :] + dot_t(nb_chunk(U - 1, i), t_u[U - 1].reshape(Wo, 2 * UNIT))
        value = value.astype(jnp.bfloat16)
        gsib[at_chunk(i), :] = dot(value, pt_sib[...]).astype(jnp.bfloat16)
        back(i).start()
        rows = pl.ds(pl.multiple_of(core * R + i * CH, 16), CH)
        out_ref[rows, :] = dot(value, pt_own[...]).astype(jnp.bfloat16)

    @pl.loop(0, NCH)
    def _(i):
        back(i).wait()

    for j in range(U):
        for whole in forms(j):
            @pl.when(sends_up(j, whole))
            def _():
                up(j, whole).wait_send()

            @pl.when(sends_down(j, whole))
            def _():
                down(j, whole).wait_send()

            if relay and has(j, edge_halves, whole):
                @pl.when(chip == 1)
                def _():
                    relay_up(j, whole).wait_send()

                @pl.when(chip == n_chip - 2)
                def _():
                    relay_down(j, whole).wait_send()


def call(n_chip, n_grp, edge_halves, inner_halves, ident, occ_count, aux_count, energy, vir, block):
    U, nv = -(-max(edge_halves, inner_halves) // 2), vir.shape[1]
    rows, C = block.shape
    R = rows // 2
    CH = chunk_rows(R // 2)
    D = 2 * n_grp
    W = U * UNIT
    S = -(-W // (D * 16)) * 16
    Wo = D * S
    N = 2 * UNIT
    dims = (n_chip, n_grp, edge_halves, inner_halves, R, CH, S, D, C, nv)
    bf, f32 = jnp.bfloat16, jnp.float32
    vm, dma = pltpu.VMEM, pltpu.SemaphoreType.DMA
    scratch = [
        vm((8, C), f32), vm((R, C), bf), vm((8, C), f32), vm((C, W), bf), vm((C, W), bf), vm((Wo, C), bf), vm((Wo, C), bf),
        vm((U, R, UNIT), bf), vm((R // 2, UNIT), bf), vm((R // CH, Wo, CH), bf), vm((8, W), f32), vm((D, S, UNIT), f32),
        vm((2, U, R, UNIT), bf), vm((2, R // 2, UNIT), bf), vm((2, 8, W), f32), vm((Wo, W), f32), vm((R, Wo), f32), vm((R, C), bf),
        vm((D, S, W), bf), vm((D, S, W), bf), vm((D, S, W), bf),
        vm((U, D, S, N), bf), vm((U, D, S, N), bf), vm((U, D, S, N), bf),
        dma((2, 2)), dma((2, U, 2)), dma((2, U, 2)), dma((2, 2)), dma((2, D, 2)), dma((U, 2, D, 2)), dma((R // CH, 2)),
    ]
    smem = pl.BlockSpec(memory_space=pltpu.SMEM)
    vmem = pl.BlockSpec(memory_space=pltpu.VMEM)
    return pl.pallas_call(
        functools.partial(kernel, dims),
        out_shape=jax.ShapeDtypeStruct((rows, C), bf),
        in_specs=[smem, smem, smem, vmem, vmem],
        out_specs=vmem,
        scratch_shapes=scratch,
        compiler_params=pltpu.CompilerParams(
            collective_id=ident, has_side_effects=True, vmem_limit_bytes=56 * 1024 * 1024),
        cost_estimate=pl.CostEstimate(flops=12 * R * W * Wo, bytes_accessed=4 * rows * C, transcendentals=0),
    )(occ_count, aux_count, energy, vir, block)


def choose(n_chip, nv, plans, occ_count):
    def kernel(occ_ref, choice_ref):
        def columns(chip):
            return (occ_ref[2 * chip] + occ_ref[2 * chip + 1]) * nv

        edge = jnp.maximum(columns(0), columns(n_chip - 1))
        inner = lax.fori_loop(1, n_chip - 1, lambda i, most: jnp.maximum(most, columns(i)), jnp.int32(0))
        choice = jnp.int32(len(plans) - 1)
        for i in reversed(range(len(plans) - 1)):
            fits = (edge * 2 <= plans[i][0] * UNIT) & (inner * 2 <= plans[i][1] * UNIT)
            choice = jnp.where(fits, jnp.int32(i), choice)
        choice_ref[0] = choice

    smem = pl.BlockSpec(memory_space=pltpu.SMEM)
    found = pl.pallas_call(kernel, out_shape=jax.ShapeDtypeStruct((1,), jnp.int32),
                           in_specs=[smem], out_specs=smem)(occ_count)
    return found[0]


def solution(mesh):
    n_chip, n_grp = mesh.shape["blk"] // 2, mesh.shape["grp"]

    def per_device(three_index, occ_energy, vir_energy, aux_count, occ_count):
        C, nv = three_index.shape[1], vir_energy.shape[0]
        full = 4 * C // UNIT
        if n_chip == 4:
            plans = [(full - 3, full - 3), (full - 2, full - 4), (full - 4, full - 2),
                     (full - 2, full - 2), (full, full - 4), (full - 4, full), (full, full)]
        else:
            plans = [(full - 3, full - 3), (full - 2, full - 2), (full - 1, full - 1), (full, full)]
        choice = choose(n_chip, nv, plans, occ_count)
        return lax.switch(
            choice,
            [functools.partial(call, n_chip, n_grp, *plan, i + 1) for i, plan in enumerate(plans)],
            occ_count, aux_count, occ_energy, vir_energy.reshape(1, nv), three_index)

    in_specs = (P("grp", "blk"), P("blk"), P(), P(), P())
    return jax.shard_map(
        per_device, mesh=mesh, in_specs=in_specs, out_specs=P("grp", "blk"), check_vma=False)
```
